32 devices in a mesh: parts: 2 (over y), wide: 8 (over z, x), narrow: 2 (over core).
Axes of the slice: x: 2, y: 2, z: 4, core: 2. Of those that a mesh axis runs over, the one named last changes fastest.
Arguments:
- signal: bfloat16 [4096, 768], P(('parts', 'wide', 'narrow')), parts along dimension 0, may hold values from -6 to 6
- gate_values: bfloat16 [4096, 768], P(('parts', 'wide', 'narrow')), parts along dimension 0, may hold values from -6 to 6
- filter_taps: bfloat16 [2048, 768], P(('wide', 'narrow')), may hold values from -1.1 to 1.1
- skip_gain: float32 [768], P(('wide', 'narrow')), may hold values from -4 to 4
- grad_output: bfloat16 [4096, 768], P(('parts', 'wide', 'narrow')), parts along dimension 0, may hold values from -6 to 6
Outputs:
- signal_grad: bfloat16 [4096, 768], P(('parts', 'wide', 'narrow')), parts along dimension 0
- gate_grad: bfloat16 [4096, 768], P(('parts', 'wide', 'narrow')), parts along dimension 0
- filter_grad: bfloat16 [4096, 768], P(('parts', 'wide', 'narrow')), parts along dimension 0
The draws below stay inside these ranges and needn't reach their ends.
There are 2 independent parts, one for each index of `parts`. The reference program is written for one: setup_inputs(seed, part) draws one part's arguments, and reference() takes and returns one part's arrays. A program takes and returns all parts, laid end to end along the dimension named above; an argument that names none is the same for every part. Nothing has to cross between parts.
All inputs are finite; a program needn't handle non-finite values.
Results may differ from the reference program's by a relative error of at most 0.0051.
Values may be sent and summed in bfloat16 or wider, within the bound.
A program may use at most 64 MiB of HBM per device.

```python
import math
import jax
import jax.numpy as jnp

CH = 768
TOKENS = 2048


def draw_filter_taps(key, part):
    key_rate = jax.random.fold_in(key, 11)
    key_jitter = jax.random.fold_in(key, 23)
    lowest = math.log(30.0)
    highest = math.log(4.0 * TOKENS)
    lifetimes = jnp.exp(jax.random.uniform(key_rate, (CH,), jnp.float32, lowest, highest))
    jitter = jnp.clip(jax.random.normal(key_jitter, (TOKENS, CH), jnp.float32), -4.0, 4.0)
    horizon = jnp.minimum(lifetimes, float(TOKENS))
    offsets = jnp.arange(TOKENS, dtype=jnp.float32)
    envelope = jnp.exp(-offsets[:, None] / lifetimes[None, :]) * jnp.sqrt(2.0 / horizon)[None, :]
    return (jitter * envelope).astype(jnp.bfloat16)


def shard_levels(key, dims, shards, smallest, top_value):
    level = 1.0
    for dim, parts in shards:
        heights = jax.random.uniform(jax.random.fold_in(jax.random.fold_in(key, 6), dim), (parts,), jnp.float32, smallest / len(shards), top_value / len(shards))
        level = level * jnp.repeat(jnp.exp(heights), dims[dim] // parts).reshape((-1,) + (1,) * (len(dims) - 1 - dim))
    return level


def scatter_about(key, shape, scale, most, split=(), kind=jnp.bfloat16):
    level = shard_levels(key, shape, split, -0.22, 0.18) if split else 1.0
    values = jax.random.normal(key, shape, jnp.float32) * scale * level
    return jnp.minimum(jnp.maximum(values, -most), most).astype(kind)


def setup_inputs(seed: int = 0, part: int = 0) -> dict:
    key_of = jax.random.split(jax.random.key(seed), 6)
    part_splits = jax.random.split(jax.random.fold_in(key_of[5], part), 6)
    signal = scatter_about(part_splits[0], (TOKENS, CH), 1.0, 6.0, ((0, 16),))
    gate_values = scatter_about(part_splits[1], (TOKENS, CH), 1.0, 6.0, ((0, 16),))
    filter_taps = draw_filter_taps(jax.random.fold_in(key_of[5], 71), part)
    skip_gain = scatter_about(key_of[3], (CH,), 1.0, 4.0, ((0, 16),), jnp.float32)
    grad_output = scatter_about(part_splits[4], (TOKENS, CH), 1.0, 6.0, ((0, 16),))
    return dict(signal=signal, gate_values=gate_values, filter_taps=filter_taps, skip_gain=skip_gain, grad_output=grad_output)


def reference(signal, gate_values, filter_taps, skip_gain, grad_output):
    length = signal.shape[0]
    padded = 2 * length
    signal_vals = signal.astype(jnp.float32)
    taps_vals = filter_taps.astype(jnp.float32)
    signal_hat = jnp.fft.rfft(signal_vals, n=padded, axis=0)
    taps_hat = jnp.fft.rfft(taps_vals, n=padded, axis=0)
    convolved = jnp.fft.irfft(signal_hat * taps_hat, n=padded, axis=0)[:length]
    mixed_out = (convolved + skip_gain[None, :] * signal_vals).astype(jnp.bfloat16)
    grad_vals = grad_output.astype(jnp.float32)
    gate_grad = (grad_vals * mixed_out.astype(jnp.float32)).astype(jnp.bfloat16)
    inner_grad = (grad_vals * gate_values.astype(jnp.float32)).astype(jnp.bfloat16)
    inner_vals = inner_grad.astype(jnp.float32)
    inner_hat = jnp.fft.rfft(inner_vals, n=padded, axis=0)
    back_taps = jnp.fft.irfft(inner_hat * jnp.conj(taps_hat), n=padded, axis=0)[:length]
    back_signal = jnp.fft.irfft(inner_hat * jnp.conj(signal_hat), n=padded, axis=0)[:length]
    signal_grad = (back_taps + skip_gain[None, :] * inner_vals).astype(jnp.bfloat16)
    filter_grad = (back_signal / math.sqrt(length)).astype(jnp.bfloat16)
    return (signal_grad, gate_grad, filter_grad)
```

```python
import functools
import math

import jax
import jax.numpy as jnp
import numpy as np
from jax import lax
from jax.experimental import pallas as pl
from jax.experimental.pallas import tpu as pltpu
from jax.sharding import PartitionSpec as P

precise = lax.Precision.HIGHEST


def angle_tables(left_count, right_count, period):
    left_index = jnp.arange(left_count, dtype=jnp.int32)
    right_index = jnp.arange(right_count, dtype=jnp.int32)
    phases = left_index[:, None] * right_index[None, :] % period
    angles = phases.astype(jnp.float32) * (2.0 * math.pi / period)
    return (jnp.cos(angles), jnp.sin(angles))


def spectral_tables(groups, seq_rows):
    full_span = 2 * groups * seq_rows
    outer_cos, outer_sin = angle_tables(2 * groups, groups, 2 * groups)
    twist_cos, twist_sin = angle_tables(2 * groups, seq_rows, full_span)
    inner_cos, inner_sin = angle_tables(seq_rows, seq_rows, seq_rows)
    return (outer_cos, outer_sin, twist_cos, twist_sin, inner_cos, inner_sin, full_span)


def transform(field, tables):
    outer_cos, outer_sin, twist_cos, twist_sin, inner_cos, inner_sin, full_span = tables
    first_real = jnp.einsum("ka,ucab->uckb", outer_cos, field, precision=precise)
    first_imag = -jnp.einsum("ka,ucab->uckb", outer_sin, field, precision=precise)
    turned_real = first_real * twist_cos + first_imag * twist_sin
    turned_imag = first_imag * twist_cos - first_real * twist_sin
    spec_real = jnp.einsum("uckb,bj->uckj", turned_real, inner_cos, precision=precise) + jnp.einsum(
        "uckb,bj->uckj", turned_imag, inner_sin, precision=precise
    )
    spec_imag = jnp.einsum("uckb,bj->uckj", turned_imag, inner_cos, precision=precise) - jnp.einsum(
        "uckb,bj->uckj", turned_real, inner_sin, precision=precise
    )
    return (spec_real, spec_imag)


def untwist(spec_real, spec_imag, tables):
    outer_cos, outer_sin, twist_cos, twist_sin, inner_cos, inner_sin, full_span = tables
    back_real = jnp.einsum("uckj,bj->uckb", spec_real, inner_cos, precision=precise) - jnp.einsum(
        "uckj,bj->uckb", spec_imag, inner_sin, precision=precise
    )
    back_imag = jnp.einsum("uckj,bj->uckb", spec_imag, inner_cos, precision=precise) + jnp.einsum(
        "uckj,bj->uckb", spec_real, inner_sin, precision=precise
    )
    turned_real = back_real * twist_cos - back_imag * twist_sin
    turned_imag = back_imag * twist_cos + back_real * twist_sin
    return (turned_real, turned_imag)


def inverse_real(spec_real, spec_imag, tables):
    outer_cos, outer_sin = (tables[0], tables[1])
    factor = 1.0 / tables[6]
    turned_real, turned_imag = untwist(spec_real, spec_imag, tables)
    out_real = jnp.einsum("ka,uckb->ucab", outer_cos, turned_real, precision=precise) - jnp.einsum(
        "ka,uckb->ucab", outer_sin, turned_imag, precision=precise
    )
    return out_real * factor


def to_channels(stacked, wide_count, narrow_count):
    stack_count, channels, seq_rows = stacked.shape
    groups = wide_count * narrow_count
    own_channels = channels // groups
    arrived = lax.all_to_all(stacked, ("wide", "narrow"), split_axis=1, concat_axis=2, tiled=True)
    return arrived.reshape(stack_count, own_channels, groups, seq_rows)


def to_sequence(field):
    stack_count, own_channels, groups, seq_rows = field.shape
    flat_field = field.reshape(stack_count, own_channels, groups * seq_rows)
    arrived = lax.all_to_all(
        flat_field, ("wide", "narrow"), split_axis=2, concat_axis=1, tiled=True
    )
    return arrived


def backward_channels(
    inner_chan,
    inner_real,
    inner_imag,
    signal_real,
    signal_imag,
    taps_real,
    taps_imag,
    skip_gain,
    tables,
    total_rows,
):
    taps_side_real = inner_real * taps_real + inner_imag * taps_imag
    taps_side_imag = inner_imag * taps_real - inner_real * taps_imag
    signal_side_real = inner_real * signal_real + inner_imag * signal_imag
    signal_side_imag = inner_imag * signal_real - inner_real * signal_imag
    back_taps = inverse_real(taps_side_real, taps_side_imag, tables)
    back_signal = inverse_real(signal_side_real, signal_side_imag, tables)
    signal_chan = (back_taps[0] + skip_gain[:, None, None] * inner_chan[0]).astype(jnp.bfloat16)
    filter_chan = (back_signal[0] * (1.0 / math.sqrt(total_rows))).astype(jnp.bfloat16)
    return (signal_chan, filter_chan)


def per_device_plain(signal, gate_values, filter_taps, skip_gain, grad_output):
    wide_count = lax.axis_size("wide")
    narrow_count = lax.axis_size("narrow")
    groups = wide_count * narrow_count
    seq_rows = signal.shape[0]
    total_rows = groups * seq_rows
    tables = spectral_tables(groups, seq_rows)
    grad_vals = grad_output.astype(jnp.float32)
    paired = jnp.stack([jnp.transpose(signal), jnp.transpose(filter_taps)])
    spread_pair = to_channels(paired, wide_count, narrow_count).astype(jnp.float32)
    pair_real, pair_imag = transform(spread_pair, tables)
    signal_real, signal_imag = (pair_real[0:1], pair_imag[0:1])
    taps_real, taps_imag = (pair_real[1:2], pair_imag[1:2])
    conv_real = signal_real * taps_real - signal_imag * taps_imag
    conv_imag = signal_real * taps_imag + signal_imag * taps_real
    convolved = inverse_real(conv_real, conv_imag, tables)[0]
    mixed_chan = (convolved + skip_gain[:, None, None] * spread_pair[0]).astype(jnp.bfloat16)
    mixed_rows = jnp.transpose(to_sequence(mixed_chan[None])[0])
    gate_grad = (grad_vals * mixed_rows.astype(jnp.float32)).astype(jnp.bfloat16)
    inner_grad = (grad_vals * gate_values.astype(jnp.float32)).astype(jnp.bfloat16)
    inner_chan = to_channels(jnp.transpose(inner_grad)[None], wide_count, narrow_count).astype(
        jnp.float32
    )
    inner_real, inner_imag = transform(inner_chan, tables)
    signal_chan, filter_chan = backward_channels(
        inner_chan,
        inner_real,
        inner_imag,
        signal_real,
        signal_imag,
        taps_real,
        taps_imag,
        skip_gain,
        tables,
        total_rows,
    )
    returned = to_sequence(jnp.stack([signal_chan, filter_chan]))
    signal_grad = jnp.transpose(returned[0])
    filter_grad = jnp.transpose(returned[1])
    return (signal_grad, gate_grad, filter_grad)


LANES = 128
CHUNK = 16
MESH = pl.DeviceIdType.MESH


def fused_tables(groups, seq_rows):
    span = 2 * groups * seq_rows
    kept = np.arange(groups + 1)[:, None]
    turn = 2.0 * np.pi * (kept * np.arange(seq_rows)[None, :]) / span
    weight = np.where((kept == 0) | (kept == groups), 1.0, 2.0) / span
    twist = np.stack([np.cos(turn), np.sin(turn), weight * np.cos(turn), weight * np.sin(turn)])
    index = np.arange(seq_rows)
    angle = 2.0 * np.pi * (index[:, None] * index[None, :] % seq_rows) / seq_rows
    cos, sin = np.cos(angle), np.sin(angle)
    ahead = np.block([[cos, -sin], [sin, cos]]).astype(np.float32)
    both = []
    for table in (ahead, ahead.T):
        high = table.astype(jnp.bfloat16)
        both += [high, (table - high.astype(np.float32)).astype(jnp.bfloat16)]
    return twist.astype(np.float32), np.stack(both)


def weighted_sum(pairs):
    by_size = {}
    for coefficient, array in pairs:
        if abs(coefficient) > 1e-9:
            key = round(abs(coefficient), 9)
            by_size.setdefault(key, (abs(coefficient), []))[1].append((coefficient > 0, array))
    total = None
    for size, members in by_size.values():
        members = sorted(members, key=lambda member: not member[0])
        positive = members[0][0]
        partial = members[0][1]
        for sign, array in members[1:]:
            partial = partial + array if sign == positive else partial - array
        factor = 1.0 if abs(size - 1.0) < 1e-9 else size
        if factor != 1.0:
            partial = partial * np.float32(factor)
        if total is None:
            total = partial if positive else -partial
        else:
            total = total + partial if positive else total - partial
    return total


def add(left, right):
    if left is None or right is None:
        return right if left is None else left
    return left + right


def sub(left, right):
    if left is None:
        return None if right is None else -right
    return left if right is None else left - right


def outer_forward(x):
    groups = len(x)
    half = groups // 2
    unit = math.pi / groups
    plus = {a: x[a] + x[groups - a] for a in range(1, half)}
    minus = {a: x[a] - x[groups - a] for a in range(1, half)}
    real, imag = [None] * (groups + 1), [None] * (groups + 1)
    for k in range(half + 1):
        even = k % 2 == 0
        cos_side, sin_side = (plus, minus) if even else (minus, plus)
        cos_parts, sin_parts = [[(1.0, x[0])], []], [[], []]
        cos_parts[half % 2].append((math.cos(unit * k * half), x[half]))
        sin_parts[half % 2].append((math.sin(unit * k * half), x[half]))
        for a in range(1, half):
            cos_parts[a % 2].append((math.cos(unit * k * a), cos_side[a]))
            sin_parts[a % 2].append((math.sin(unit * k * a), sin_side[a]))
        cos_even, cos_odd = weighted_sum(cos_parts[0]), weighted_sum(cos_parts[1])
        sin_even, sin_odd = weighted_sum(sin_parts[0]), weighted_sum(sin_parts[1])
        real[k] = add(cos_even, cos_odd)
        imag[k] = sub(sub(None, sin_even), sin_odd)
        real[groups - k] = sub(cos_even, cos_odd)
        if k < half:
            imag[groups - k] = sub(sin_even, sin_odd)
    zero = jnp.zeros_like(x[0])
    return [zero if v is None else v for v in real], [zero if v is None else v for v in imag]


def outer_inverse(real, imag):
    groups = len(real) - 1
    half = groups // 2
    unit = math.pi / groups
    out = [None] * groups
    for a_parity in (0, 1):
        cos_side, sin_side = {}, {}
        for k in range(1, half):
            if a_parity == 0:
                cos_side[k] = real[k] + real[groups - k]
                sin_side[k] = imag[k] - imag[groups - k]
            else:
                cos_side[k] = real[k] - real[groups - k]
                sin_side[k] = imag[k] + imag[groups - k]
        ends = real[0] + real[groups] if a_parity == 0 else real[0] - real[groups]
        for a in range(a_parity, half + 1, 2):
            cos_parts, sin_parts = [[(1.0, ends)], []], [[], []]
            cos_parts[half % 2].append((math.cos(unit * half * a), real[half]))
            sin_parts[half % 2].append((math.sin(unit * half * a), imag[half]))
            for k in range(1, half):
                cos_parts[k % 2].append((math.cos(unit * k * a), cos_side[k]))
                sin_parts[k % 2].append((math.sin(unit * k * a), sin_side[k]))
            cos_even, cos_odd = weighted_sum(cos_parts[0]), weighted_sum(cos_parts[1])
            sin_even, sin_odd = weighted_sum(sin_parts[0]), weighted_sum(sin_parts[1])
            out[a] = sub(sub(add(cos_even, cos_odd), sin_even), sin_odd)
            if 0 < a < half:
                out[groups - a] = sub(add(sub(cos_even, cos_odd), sin_even), sin_odd)
    return out


def split(value):
    high = value.astype(jnp.bfloat16)
    return high, (value - high.astype(jnp.float32)).astype(jnp.bfloat16)


def fused_kernel(
    groups,
    narrow_count,
    total_rows,
    signal_ref,
    gate_ref,
    taps_ref,
    skip_ref,
    grad_ref,
    twist_ref,
    inner_ref,
    signal_out,
    gate_out,
    filter_out,
    outgoing,
    arrived,
    results,
    returned,
    high_ref,
    low_ref,
    spec_ref,
    out_send,
    out_recv,
    back_send,
    back_recv,
    local_sem,
):
    seq_rows, channels = signal_ref.shape
    own = channels // groups
    chunks = own // CHUNK
    part = lax.axis_index("parts")
    me = lax.axis_index("wide") * narrow_count + lax.axis_index("narrow")

    def device(index):
        return (part, index // narrow_count, index % narrow_count)

    barrier = pltpu.get_barrier_semaphore()

    def greet(step, carry):
        pl.semaphore_signal(
            barrier, inc=1, device_id=device((me + step) % groups), device_id_type=MESH
        )
        return carry

    lax.fori_loop(1, groups, greet, 0)

    for first in range(0, channels, LANES):
        columns = slice(first, first + LANES)
        grad_vals = grad_ref[:, columns].astype(jnp.float32)
        inner = (grad_vals * gate_ref[:, columns].astype(jnp.float32)).astype(jnp.bfloat16)
        outgoing[0, columns, :] = signal_ref[:, columns].T
        outgoing[1, columns, :] = taps_ref[:, columns].T
        outgoing[2, columns, :] = inner.T
    pl.semaphore_wait(barrier, groups - 1)

    def rows_of(index, chunk):
        return pl.ds(pl.multiple_of(index * own + chunk * CHUNK, CHUNK), CHUNK)

    def chunk_rows(chunk):
        return pl.ds(pl.multiple_of(chunk * CHUNK, CHUNK), CHUNK)

    def spread(chunk, step):
        other = (me + step) % groups
        return pltpu.make_async_remote_copy(
            src_ref=outgoing.at[:, rows_of(other, chunk), :],
            dst_ref=arrived.at[me, :, chunk_rows(chunk), :],
            send_sem=out_send.at[chunk, step],
            recv_sem=out_recv.at[chunk, step],
            device_id=device(other),
            device_id_type=MESH,
        )

    def bring(chunk, step):
        other = (me + step) % groups
        return pltpu.make_async_remote_copy(
            src_ref=results.at[other, :, chunk_rows(chunk), :],
            dst_ref=returned.at[:, rows_of(me, chunk), :],
            send_sem=back_send.at[chunk, step],
            recv_sem=back_recv.at[chunk, step],
            device_id=device(other),
            device_id_type=MESH,
        )

    for chunk in range(chunks):

        def start(step, carry, chunk=chunk):
            spread(chunk, step).start()
            return carry

        lax.fori_loop(1, groups, start, 0)
    keep = pltpu.make_async_copy(
        outgoing.at[:, pl.ds(pl.multiple_of(me * own, CHUNK), own), :],
        arrived.at[me],
        local_sem,
    )
    keep.start()

    lane = lax.broadcasted_iota(jnp.int32, (own, own), 1)
    row = lax.broadcasted_iota(jnp.int32, (own, own), 0)
    gain_all = jnp.sum(
        jnp.where(lane == row, jnp.broadcast_to(skip_ref[...], (own, own)), 0.0),
        axis=1,
        keepdims=True,
    )
    keep.wait()

    kept = groups + 1
    size = kept * 3 * CHUNK

    def inner_transform(which):
        high = high_ref[...].reshape(size, 2 * seq_rows)
        low = low_ref[...].reshape(size, 2 * seq_rows)
        table_high, table_low = inner_ref[which], inner_ref[which + 1]
        dot = functools.partial(jnp.dot, preferred_element_type=jnp.float32)
        total = dot(high, table_high) + dot(high, table_low) + dot(low, table_high)
        spec_ref[...] = total.reshape(kept, 3, CHUNK, 2 * seq_rows)

    def store_pair(k, u, real, imag):
        real_high, real_low = split(real)
        imag_high, imag_low = split(imag)
        high_ref[k, u, :, :seq_rows] = real_high
        high_ref[k, u, :, seq_rows:] = imag_high
        low_ref[k, u, :, :seq_rows] = real_low
        low_ref[k, u, :, seq_rows:] = imag_low

    for chunk in range(chunks):
        rows = slice(chunk * CHUNK, (chunk + 1) * CHUNK)

        def await_in(step, carry, chunk=chunk):
            spread(chunk, step).wait_recv()
            return carry

        lax.fori_loop(1, groups, await_in, 0)

        def ahead(u, carry, rows=rows):
            blocks = [arrived[a, u, rows, :].astype(jnp.float32) for a in range(groups)]
            real, imag = outer_forward(blocks)
            for k in range(kept):
                cos, sin = twist_ref[0, k : k + 1, :], twist_ref[1, k : k + 1, :]
                store_pair(
                    k, u, real[k] * cos + imag[k] * sin, imag[k] * cos - real[k] * sin
                )
            return carry

        lax.fori_loop(0, 3, ahead, 0)
        inner_transform(0)

        def multiply(k, carry):
            parts = [
                (spec_ref[k, u, :, :seq_rows], spec_ref[k, u, :, seq_rows:]) for u in range(3)
            ]
            (s_re, s_im), (t_re, t_im), (i_re, i_im) = parts
            store_pair(k, 0, s_re * t_re - s_im * t_im, s_re * t_im + s_im * t_re)
            store_pair(k, 1, i_re * t_re + i_im * t_im, i_im * t_re - i_re * t_im)
            store_pair(k, 2, i_re * s_re + i_im * s_im, i_im * s_re - i_re * s_im)
            return carry

        lax.fori_loop(0, kept, multiply, 0)
        inner_transform(2)

        gain = gain_all[rows, :]

        def back(u, carry, rows=rows, gain=gain):
            real, imag = [], []
            for k in range(kept):
                re, im = spec_ref[k, u, :, :seq_rows], spec_ref[k, u, :, seq_rows:]
                cos, sin = twist_ref[2, k : k + 1, :], twist_ref[3, k : k + 1, :]
                real.append(re * cos - im * sin)
                imag.append(im * cos + re * sin)
            for a, block in enumerate(outer_inverse(real, imag)):
                skipped = arrived[a, 2 * u, rows, :].astype(jnp.float32)
                results[a, u, rows, :] = (block + gain * skipped).astype(jnp.bfloat16)
            return carry

        lax.fori_loop(0, 2, back, 0)
        real, imag = [], []
        for k in range(kept):
            re, im = spec_ref[k, 2, :, :seq_rows], spec_ref[k, 2, :, seq_rows:]
            cos, sin = twist_ref[2, k : k + 1, :], twist_ref[3, k : k + 1, :]
            real.append(re * cos - im * sin)
            imag.append(im * cos + re * sin)
        for a, block in enumerate(outer_inverse(real, imag)):
            scaled = block * np.float32(1.0 / math.sqrt(total_rows))
            results[a, 2, rows, :] = scaled.astype(jnp.bfloat16)

        def start_back(step, carry, chunk=chunk):
            bring(chunk, step).start()
            return carry

        lax.fori_loop(1, groups, start_back, 0)

    mine = pltpu.make_async_copy(
        results.at[me],
        returned.at[:, pl.ds(pl.multiple_of(me * own, CHUNK), own), :],
        local_sem,
    )
    mine.start()
    mine.wait()
    for chunk in range(chunks):

        def finish(step, carry, chunk=chunk):
            bring(chunk, step).wait_recv()
            return carry

        lax.fori_loop(1, groups, finish, 0)

    for first in range(0, channels, LANES):
        columns = slice(first, first + LANES)
        mixed = returned[0, columns, :].T.astype(jnp.float32)
        gate_out[:, columns] = (grad_ref[:, columns].astype(jnp.float32) * mixed).astype(
            jnp.bfloat16
        )
        signal_out[:, columns] = returned[1, columns, :].T
        filter_out[:, columns] = returned[2, columns, :].T

    for chunk in range(chunks):

        def drain(step, carry, chunk=chunk):
            spread(chunk, step).wait_send()
            bring(chunk, step).wait_send()
            return carry

        lax.fori_loop(1, groups, drain, 0)


def per_device_fused(signal, gate_values, filter_taps, skip_gain, grad_output):
    narrow_count = lax.axis_size("narrow")
    groups = lax.axis_size("wide") * narrow_count
    seq_rows, channels = signal.shape
    own = channels // groups
    chunks = own // CHUNK
    twist, inner = fused_tables(groups, seq_rows)
    vmem = pl.BlockSpec(memory_space=pltpu.VMEM)
    shape = jax.ShapeDtypeStruct((seq_rows, channels), jnp.bfloat16)
    rows = (groups + 1, 3, CHUNK, 2 * seq_rows)
    return pl.pallas_call(
        functools.partial(fused_kernel, groups, narrow_count, groups * seq_rows),
        out_shape=(shape, shape, shape),
        in_specs=[vmem] * 7,
        out_specs=(vmem, vmem, vmem),
        scratch_shapes=[
            pltpu.VMEM((3, channels, seq_rows), jnp.bfloat16),
            pltpu.VMEM((groups, 3, own, seq_rows), jnp.bfloat16),
            pltpu.VMEM((groups, 3, own, seq_rows), jnp.bfloat16),
            pltpu.VMEM((3, channels, seq_rows), jnp.bfloat16),
            pltpu.VMEM(rows, jnp.bfloat16),
            pltpu.VMEM(rows, jnp.bfloat16),
            pltpu.VMEM(rows, jnp.float32),
            pltpu.SemaphoreType.DMA((chunks, groups)),
            pltpu.SemaphoreType.DMA((chunks, groups)),
            pltpu.SemaphoreType.DMA((chunks, groups)),
            pltpu.SemaphoreType.DMA((chunks, groups)),
            pltpu.SemaphoreType.DMA,
        ],
        compiler_params=pltpu.CompilerParams(
            collective_id=0, has_side_effects=True, vmem_limit_bytes=40 * 1024 * 1024
        ),
    )(
        signal,
        gate_values,
        filter_taps,
        skip_gain[None, :],
        grad_output,
        jnp.asarray(twist),
        jnp.asarray(inner),
    )


def per_device(signal, gate_values, filter_taps, skip_gain, grad_output):
    groups = lax.axis_size("wide") * lax.axis_size("narrow")
    seq_rows, channels = signal.shape
    own = channels // groups
    fits = groups <= 32 and groups % 4 == 0 and seq_rows == LANES
    if fits and own >= CHUNK and own % CHUNK == 0 and channels % LANES == 0:
        return per_device_fused(signal, gate_values, filter_taps, skip_gain, grad_output)
    return per_device_plain(signal, gate_values, filter_taps, skip_gain, grad_output)


def solution(mesh):
    placed = (
        P(("parts", "wide", "narrow"), None),
        P(("parts", "wide", "narrow"), None),
        P(("wide", "narrow"), None),
        P(("wide", "narrow")),
        P(("parts", "wide", "narrow"), None),
    )
    return jax.shard_map(
        per_device,
        mesh=mesh,
        in_specs=placed,
        out_specs=(
            P(("parts", "wide", "narrow"), None),
            P(("parts", "wide", "narrow"), None),
            P(("parts", "wide", "narrow"), None),
        ),
        check_vma=False,
    )
```

```python
import functools
import math

import jax
import jax.numpy as jnp
import numpy as np
from jax import lax
from jax.experimental import pallas as pl
from jax.experimental.pallas import tpu as pltpu
from jax.sharding import PartitionSpec as P

precise = lax.Precision.HIGHEST


def angle_tables(left_count, right_count, period):
    left_index = jnp.arange(left_count, dtype=jnp.int32)
    right_index = jnp.arange(right_count, dtype=jnp.int32)
    phases = left_index[:, None] * right_index[None, :] % period
    angles = phases.astype(jnp.float32) * (2.0 * math.pi / period)
    return (jnp.cos(angles), jnp.sin(angles))


def spectral_tables(groups, seq_rows):
    full_span = 2 * groups * seq_rows
    outer_cos, outer_sin = angle_tables(2 * groups, groups, 2 * groups)
    twist_cos, twist_sin = angle_tables(2 * groups, seq_rows, full_span)
    inner_cos, inner_sin = angle_tables(seq_rows, seq_rows, seq_rows)
    return (outer_cos, outer_sin, twist_cos, twist_sin, inner_cos, inner_sin, full_span)


def transform(field, tables):
    outer_cos, outer_sin, twist_cos, twist_sin, inner_cos, inner_sin, full_span = tables
    first_real = jnp.einsum("ka,ucab->uckb", outer_cos, field, precision=precise)
    first_imag = -jnp.einsum("ka,ucab->uckb", outer_sin, field, precision=precise)
    turned_real = first_real * twist_cos + first_imag * twist_sin
    turned_imag = first_imag * twist_cos - first_real * twist_sin
    spec_real = jnp.einsum("uckb,bj->uckj", turned_real, inner_cos, precision=precise) + jnp.einsum(
        "uckb,bj->uckj", turned_imag, inner_sin, precision=precise
    )
    spec_imag = jnp.einsum("uckb,bj->uckj", turned_imag, inner_cos, precision=precise) - jnp.einsum(
        "uckb,bj->uckj", turned_real, inner_sin, precision=precise
    )
    return (spec_real, spec_imag)


def untwist(spec_real, spec_imag, tables):
    outer_cos, outer_sin, twist_cos, twist_sin, inner_cos, inner_sin, full_span = tables
    back_real = jnp.einsum("uckj,bj->uckb", spec_real, inner_cos, precision=precise) - jnp.einsum(
        "uckj,bj->uckb", spec_imag, inner_sin, precision=precise
    )
    back_imag = jnp.einsum("uckj,bj->uckb", spec_imag, inner_cos, precision=precise) + jnp.einsum(
        "uckj,bj->uckb", spec_real, inner_sin, precision=precise
    )
    turned_real = back_real * twist_cos - back_imag * twist_sin
    turned_imag = back_imag * twist_cos + back_real * twist_sin
    return (turned_real, turned_imag)


def inverse_real(spec_real, spec_imag, tables):
    outer_cos, outer_sin = (tables[0], tables[1])
    factor = 1.0 / tables[6]
    turned_real, turned_imag = untwist(spec_real, spec_imag, tables)
    out_real = jnp.einsum("ka,uckb->ucab", outer_cos, turned_real, precision=precise) - jnp.einsum(
        "ka,uckb->ucab", outer_sin, turned_imag, precision=precise
    )
    return out_real * factor


def to_channels(stacked, wide_count, narrow_count):
    stack_count, channels, seq_rows = stacked.shape
    groups = wide_count * narrow_count
    own_channels = channels // groups
    arrived = lax.all_to_all(stacked, ("wide", "narrow"), split_axis=1, concat_axis=2, tiled=True)
    return arrived.reshape(stack_count, own_channels, groups, seq_rows)


def to_sequence(field):
    stack_count, own_channels, groups, seq_rows = field.shape
    flat_field = field.reshape(stack_count, own_channels, groups * seq_rows)
    arrived = lax.all_to_all(
        flat_field, ("wide", "narrow"), split_axis=2, concat_axis=1, tiled=True
    )
    return arrived


def backward_channels(
    inner_chan,
    inner_real,
    inner_imag,
    signal_real,
    signal_imag,
    taps_real,
    taps_imag,
    skip_gain,
    tables,
    total_rows,
):
    taps_side_real = inner_real * taps_real + inner_imag * taps_imag
    taps_side_imag = inner_imag * taps_real - inner_real * taps_imag
    signal_side_real = inner_real * signal_real + inner_imag * signal_imag
    signal_side_imag = inner_imag * signal_real - inner_real * signal_imag
    back_taps = inverse_real(taps_side_real, taps_side_imag, tables)
    back_signal = inverse_real(signal_side_real, signal_side_imag, tables)
    signal_chan = (back_taps[0] + skip_gain[:, None, None] * inner_chan[0]).astype(jnp.bfloat16)
    filter_chan = (back_signal[0] * (1.0 / math.sqrt(total_rows))).astype(jnp.bfloat16)
    return (signal_chan, filter_chan)


def per_device_plain(signal, gate_values, filter_taps, skip_gain, grad_output):
    wide_count = lax.axis_size("wide")
    narrow_count = lax.axis_size("narrow")
    groups = wide_count * narrow_count
    seq_rows = signal.shape[0]
    total_rows = groups * seq_rows
    tables = spectral_tables(groups, seq_rows)
    grad_vals = grad_output.astype(jnp.float32)
    paired = jnp.stack([jnp.transpose(signal), jnp.transpose(filter_taps)])
    spread_pair = to_channels(paired, wide_count, narrow_count).astype(jnp.float32)
    pair_real, pair_imag = transform(spread_pair, tables)
    signal_real, signal_imag = (pair_real[0:1], pair_imag[0:1])
    taps_real, taps_imag = (pair_real[1:2], pair_imag[1:2])
    conv_real = signal_real * taps_real - signal_imag * taps_imag
    conv_imag = signal_real * taps_imag + signal_imag * taps_real
    convolved = inverse_real(conv_real, conv_imag, tables)[0]
    mixed_chan = (convolved + skip_gain[:, None, None] * spread_pair[0]).astype(jnp.bfloat16)
    mixed_rows = jnp.transpose(to_sequence(mixed_chan[None])[0])
    gate_grad = (grad_vals * mixed_rows.astype(jnp.float32)).astype(jnp.bfloat16)
    inner_grad = (grad_vals * gate_values.astype(jnp.float32)).astype(jnp.bfloat16)
    inner_chan = to_channels(jnp.transpose(inner_grad)[None], wide_count, narrow_count).astype(
        jnp.float32
    )
    inner_real, inner_imag = transform(inner_chan, tables)
    signal_chan, filter_chan = backward_channels(
        inner_chan,
        inner_real,
        inner_imag,
        signal_real,
        signal_imag,
        taps_real,
        taps_imag,
        skip_gain,
        tables,
        total_rows,
    )
    returned = to_sequence(jnp.stack([signal_chan, filter_chan]))
    signal_grad = jnp.transpose(returned[0])
    filter_grad = jnp.transpose(returned[1])
    return (signal_grad, gate_grad, filter_grad)


LANES = 128
CHUNK = 16
MESH = pl.DeviceIdType.MESH


def fused_tables(groups, seq_rows):
    span = 2 * groups * seq_rows
    kept = np.arange(groups + 1)[:, None]
    turn = 2.0 * np.pi * (kept * np.arange(seq_rows)[None, :]) / span
    weight = np.where((kept == 0) | (kept == groups), 1.0, 2.0) / span
    twist = np.stack([np.cos(turn), np.sin(turn), weight * np.cos(turn), weight * np.sin(turn)])
    index = np.arange(seq_rows)
    angle = 2.0 * np.pi * (index[:, None] * index[None, :] % seq_rows) / seq_rows
    cos, sin = np.cos(angle), np.sin(angle)
    ahead = np.block([[cos, -sin], [sin, cos]]).astype(np.float32)
    both = []
    for table in (ahead, ahead.T):
        high = table.astype(jnp.bfloat16)
        both += [high, (table - high.astype(np.float32)).astype(jnp.bfloat16)]
    return twist.astype(np.float32), np.stack(both)


def weighted_sum(pairs):
    by_size = {}
    for coefficient, array in pairs:
        if abs(coefficient) > 1e-9:
            key = round(abs(coefficient), 9)
            by_size.setdefault(key, (abs(coefficient), []))[1].append((coefficient > 0, array))
    total = None
    for size, members in by_size.values():
        members = sorted(members, key=lambda member: not member[0])
        positive = members[0][0]
        partial = members[0][1]
        for sign, array in members[1:]:
            partial = partial + array if sign == positive else partial - array
        factor = 1.0 if abs(size - 1.0) < 1e-9 else size
        if factor != 1.0:
            partial = partial * np.float32(factor)
        if total is None:
            total = partial if positive else -partial
        else:
            total = total + partial if positive else total - partial
    return total


def add(left, right):
    if left is None or right is None:
        return right if left is None else left
    return left + right


def sub(left, right):
    if left is None:
        return None if right is None else -right
    return left if right is None else left - right


def outer_forward(x):
    groups = len(x)
    half = groups // 2
    unit = math.pi / groups
    plus = {a: x[a] + x[groups - a] for a in range(1, half)}
    minus = {a: x[a] - x[groups - a] for a in range(1, half)}
    real, imag = [None] * (groups + 1), [None] * (groups + 1)
    for k in range(half + 1):
        even = k % 2 == 0
        cos_side, sin_side = (plus, minus) if even else (minus, plus)
        cos_parts, sin_parts = [[(1.0, x[0])], []], [[], []]
        cos_parts[half % 2].append((math.cos(unit * k * half), x[half]))
        sin_parts[half % 2].append((math.sin(unit * k * half), x[half]))
        for a in range(1, half):
            cos_parts[a % 2].append((math.cos(unit * k * a), cos_side[a]))
            sin_parts[a % 2].append((math.sin(unit * k * a), sin_side[a]))
        cos_even, cos_odd = weighted_sum(cos_parts[0]), weighted_sum(cos_parts[1])
        sin_even, sin_odd = weighted_sum(sin_parts[0]), weighted_sum(sin_parts[1])
        real[k] = add(cos_even, cos_odd)
        imag[k] = sub(sub(None, sin_even), sin_odd)
        real[groups - k] = sub(cos_even, cos_odd)
        if k < half:
            imag[groups - k] = sub(sin_even, sin_odd)
    zero = jnp.zeros_like(x[0])
    return [zero if v is None else v for v in real], [zero if v is None else v for v in imag]


def outer_inverse(real, imag):
    groups = len(real) - 1
    half = groups // 2
    unit = math.pi / groups
    out = [None] * groups
    for a_parity in (0, 1):
        cos_side, sin_side = {}, {}
        for k in range(1, half):
            if a_parity == 0:
                cos_side[k] = real[k] + real[groups - k]
                sin_side[k] = imag[k] - imag[groups - k]
            else:
                cos_side[k] = real[k] - real[groups - k]
                sin_side[k] = imag[k] + imag[groups - k]
        ends = real[0] + real[groups] if a_parity == 0 else real[0] - real[groups]
        for a in range(a_parity, half + 1, 2):
            cos_parts, sin_parts = [[(1.0, ends)], []], [[], []]
            cos_parts[half % 2].append((math.cos(unit * half * a), real[half]))
            sin_parts[half % 2].append((math.sin(unit * half * a), imag[half]))
            for k in range(1, half):
                cos_parts[k % 2].append((math.cos(unit * k * a), cos_side[k]))
                sin_parts[k % 2].append((math.sin(unit * k * a), sin_side[k]))
            cos_even, cos_odd = weighted_sum(cos_parts[0]), weighted_sum(cos_parts[1])
            sin_even, sin_odd = weighted_sum(sin_parts[0]), weighted_sum(sin_parts[1])
            out[a] = sub(sub(add(cos_even, cos_odd), sin_even), sin_odd)
            if 0 < a < half:
                out[groups - a] = sub(add(sub(cos_even, cos_odd), sin_even), sin_odd)
    return out


def split(value):
    high = value.astype(jnp.bfloat16)
    return high, (value - high.astype(jnp.float32)).astype(jnp.bfloat16)


def fused_kernel(
    groups,
    narrow_count,
    total_rows,
    signal_hbm,
    gate_hbm,
    taps_hbm,
    skip_hbm,
    grad_hbm,
    twist_hbm,
    inner_hbm,
    returned,
    signal_ref,
    gate_ref,
    taps_ref,
    skip_ref,
    grad_ref,
    twist_ref,
    inner_ref,
    outgoing,
    arrived,
    results,
    high_ref,
    low_ref,
    spec_ref,
    out_send,
    out_recv,
    back_send,
    back_recv,
    local_sem,
    load_sem,
):
    seq_rows, channels = signal_ref.shape
    own = channels // groups
    chunks = own // CHUNK
    part = lax.axis_index("parts")
    me = lax.axis_index("wide") * narrow_count + lax.axis_index("narrow")

    def device(index):
        return (part, index // narrow_count, index % narrow_count)

    barrier = pltpu.get_barrier_semaphore()
    pairs = [
        (signal_hbm, signal_ref),
        (taps_hbm, taps_ref),
        (grad_hbm, grad_ref),
        (gate_hbm, gate_ref),
        (skip_hbm, skip_ref),
        (twist_hbm, twist_ref),
        (inner_hbm, inner_ref),
    ]
    loads = [
        pltpu.make_async_copy(far, near, load_sem.at[i]) for i, (far, near) in enumerate(pairs)
    ]
    for load in loads:
        load.start()

    def greet(step, carry):
        pl.semaphore_signal(
            barrier, inc=1, device_id=device((me + step) % groups), device_id_type=MESH
        )
        return carry

    lax.fori_loop(1, groups, greet, 0)

    for load in loads[:4]:
        load.wait()
    for first in range(0, channels, LANES):
        columns = slice(first, first + LANES)
        grad_vals = grad_ref[:, columns].astype(jnp.float32)
        inner = (grad_vals * gate_ref[:, columns].astype(jnp.float32)).astype(jnp.bfloat16)
        outgoing[0, columns, :] = signal_ref[:, columns].T
        outgoing[1, columns, :] = taps_ref[:, columns].T
        outgoing[2, columns, :] = inner.T
    pl.semaphore_wait(barrier, groups - 1)

    def rows_of(index, chunk):
        return pl.ds(pl.multiple_of(index * own + chunk * CHUNK, CHUNK), CHUNK)

    def chunk_rows(chunk):
        return pl.ds(pl.multiple_of(chunk * CHUNK, CHUNK), CHUNK)

    def spread(chunk, step):
        other = (me + step) % groups
        return pltpu.make_async_remote_copy(
            src_ref=outgoing.at[:, rows_of(other, chunk), :],
            dst_ref=arrived.at[me, :, chunk_rows(chunk), :],
            send_sem=out_send.at[chunk, step],
            recv_sem=out_recv.at[chunk, step],
            device_id=device(other),
            device_id_type=MESH,
        )

    def bring(chunk, step):
        other = (me + step) % groups
        return pltpu.make_async_remote_copy(
            src_ref=results.at[other, :, chunk_rows(chunk), :],
            dst_ref=returned.at[:, rows_of(me, chunk), :],
            send_sem=back_send.at[chunk, step],
            recv_sem=back_recv.at[chunk, step],
            device_id=device(other),
            device_id_type=MESH,
        )

    for chunk in range(chunks):

        def start(step, carry, chunk=chunk):
            spread(chunk, step).start()
            return carry

        lax.fori_loop(1, groups, start, 0)
    keep = pltpu.make_async_copy(
        outgoing.at[:, pl.ds(pl.multiple_of(me * own, CHUNK), own), :],
        arrived.at[me],
        local_sem,
    )
    keep.start()

    for load in loads[4:]:
        load.wait()
    lane = lax.broadcasted_iota(jnp.int32, (own, own), 1)
    row = lax.broadcasted_iota(jnp.int32, (own, own), 0)
    gain_all = jnp.sum(
        jnp.where(lane == row, jnp.broadcast_to(skip_ref[...], (own, own)), 0.0),
        axis=1,
        keepdims=True,
    )
    keep.wait()

    kept = groups + 1
    size = kept * 3 * CHUNK

    def inner_transform(which):
        high = high_ref[...].reshape(size, 2 * seq_rows)
        low = low_ref[...].reshape(size, 2 * seq_rows)
        table_high, table_low = inner_ref[which], inner_ref[which + 1]
        dot = functools.partial(jnp.dot, preferred_element_type=jnp.float32)
        total = dot(high, table_high) + dot(high, table_low) + dot(low, table_high)
        spec_ref[...] = total.reshape(kept, 3, CHUNK, 2 * seq_rows)

    def store_pair(k, u, real, imag):
        real_high, real_low = split(real)
        imag_high, imag_low = split(imag)
        high_ref[k, u, :, :seq_rows] = real_high
        high_ref[k, u, :, seq_rows:] = imag_high
        low_ref[k, u, :, :seq_rows] = real_low
        low_ref[k, u, :, seq_rows:] = imag_low

    for chunk in range(chunks):
        rows = slice(chunk * CHUNK, (chunk + 1) * CHUNK)

        def await_in(step, carry, chunk=chunk):
            spread(chunk, step).wait_recv()
            return carry

        lax.fori_loop(1, groups, await_in, 0)

        def ahead(u, carry, rows=rows):
            blocks = [arrived[a, u, rows, :].astype(jnp.float32) for a in range(groups)]
            real, imag = outer_forward(blocks)
            for k in range(kept):
                cos, sin = twist_ref[0, k : k + 1, :], twist_ref[1, k : k + 1, :]
                store_pair(
                    k, u, real[k] * cos + imag[k] * sin, imag[k] * cos - real[k] * sin
                )
            return carry

        lax.fori_loop(0, 3, ahead, 0)
        inner_transform(0)

        def multiply(k, carry):
            parts = [
                (spec_ref[k, u, :, :seq_rows], spec_ref[k, u, :, seq_rows:]) for u in range(3)
            ]
            (s_re, s_im), (t_re, t_im), (i_re, i_im) = parts
            store_pair(k, 0, s_re * t_re - s_im * t_im, s_re * t_im + s_im * t_re)
            store_pair(k, 1, i_re * t_re + i_im * t_im, i_im * t_re - i_re * t_im)
            store_pair(k, 2, i_re * s_re + i_im * s_im, i_im * s_re - i_re * s_im)
            return carry

        lax.fori_loop(0, kept, multiply, 0)
        inner_transform(2)

        gain = gain_all[rows, :]

        def back(u, carry, rows=rows, gain=gain):
            real, imag = [], []
            for k in range(kept):
                re, im = spec_ref[k, u, :, :seq_rows], spec_ref[k, u, :, seq_rows:]
                cos, sin = twist_ref[2, k : k + 1, :], twist_ref[3, k : k + 1, :]
                real.append(re * cos - im * sin)
                imag.append(im * cos + re * sin)
            for a, block in enumerate(outer_inverse(real, imag)):
                skipped = arrived[a, 2 * u, rows, :].astype(jnp.float32)
                results[a, u, rows, :] = (block + gain * skipped).astype(jnp.bfloat16)
            return carry

        lax.fori_loop(0, 2, back, 0)
        real, imag = [], []
        for k in range(kept):
            re, im = spec_ref[k, 2, :, :seq_rows], spec_ref[k, 2, :, seq_rows:]
            cos, sin = twist_ref[2, k : k + 1, :], twist_ref[3, k : k + 1, :]
            real.append(re * cos - im * sin)
            imag.append(im * cos + re * sin)
        for a, block in enumerate(outer_inverse(real, imag)):
            scaled = block * np.float32(1.0 / math.sqrt(total_rows))
            results[a, 2, rows, :] = scaled.astype(jnp.bfloat16)

        def start_back(step, carry, chunk=chunk):
            bring(chunk, step).start()
            return carry

        lax.fori_loop(1, groups, start_back, 0)

    mine = pltpu.make_async_copy(
        results.at[me],
        returned.at[:, pl.ds(pl.multiple_of(me * own, CHUNK), own), :],
        local_sem,
    )
    mine.start()
    mine.wait()
    for chunk in range(chunks):

        def finish(step, carry, chunk=chunk):
            bring(chunk, step).wait_recv()
            return carry

        lax.fori_loop(1, groups, finish, 0)

    for chunk in range(chunks):

        def drain(step, carry, chunk=chunk):
            spread(chunk, step).wait_send()
            bring(chunk, step).wait_send()
            return carry

        lax.fori_loop(1, groups, drain, 0)


def tokens_kernel(
    returned_hbm,
    grad_hbm,
    signal_out,
    gate_out,
    filter_out,
    returned,
    grad_ref,
    staged,
    load_sems,
    sems,
):
    outs = (signal_out, gate_out, filter_out)
    copies = []
    spans = [slice(first, first + LANES) for first in range(0, grad_ref.shape[1], LANES)]
    grad_load = pltpu.make_async_copy(grad_hbm, grad_ref, load_sems.at[len(spans)])
    grad_load.start()
    loads = [
        pltpu.make_async_copy(
            returned_hbm.at[:, columns, :], returned.at[:, columns, :], load_sems.at[block]
        )
        for block, columns in enumerate(spans)
    ]
    for load in loads:
        load.start()
    grad_load.wait()
    for block, columns in enumerate(spans):
        loads[block].wait()
        mixed = returned[0, columns, :].T.astype(jnp.float32)
        staged[0, :, columns] = returned[1, columns, :].T
        staged[1, :, columns] = (grad_ref[:, columns].astype(jnp.float32) * mixed).astype(
            jnp.bfloat16
        )
        staged[2, :, columns] = returned[2, columns, :].T
        for u in range(3):
            copies.append(
                pltpu.make_async_copy(
                    staged.at[u, :, columns], outs[u].at[:, columns], sems.at[block, u]
                )
            )
            copies[-1].start()
    for copy in copies:
        copy.wait()


def per_device_fused(signal, gate_values, filter_taps, skip_gain, grad_output):
    narrow_count = lax.axis_size("narrow")
    groups = lax.axis_size("wide") * narrow_count
    seq_rows, channels = signal.shape
    own = channels // groups
    chunks = own // CHUNK
    twist, inner = fused_tables(groups, seq_rows)
    far = pl.BlockSpec(memory_space=pl.ANY)
    rows = (groups + 1, 3, CHUNK, 2 * seq_rows)
    operands = (
        signal,
        gate_values,
        filter_taps,
        skip_gain[None, :],
        grad_output,
        jnp.asarray(twist),
        jnp.asarray(inner),
    )
    returned = pl.pallas_call(
        functools.partial(fused_kernel, groups, narrow_count, groups * seq_rows),
        out_shape=jax.ShapeDtypeStruct((3, channels, seq_rows), jnp.bfloat16),
        in_specs=[far] * len(operands),
        out_specs=far,
        scratch_shapes=[
            *[pltpu.VMEM(operand.shape, operand.dtype) for operand in operands],
            pltpu.VMEM((3, channels, seq_rows), jnp.bfloat16),
            pltpu.VMEM((groups, 3, own, seq_rows), jnp.bfloat16),
            pltpu.VMEM((groups, 3, own, seq_rows), jnp.bfloat16),
            pltpu.VMEM(rows, jnp.bfloat16),
            pltpu.VMEM(rows, jnp.bfloat16),
            pltpu.VMEM(rows, jnp.float32),
            pltpu.SemaphoreType.DMA((chunks, groups)),
            pltpu.SemaphoreType.DMA((chunks, groups)),
            pltpu.SemaphoreType.DMA((chunks, groups)),
            pltpu.SemaphoreType.DMA((chunks, groups)),
            pltpu.SemaphoreType.DMA,
            pltpu.SemaphoreType.DMA((len(operands),)),
        ],
        compiler_params=pltpu.CompilerParams(
            collective_id=0, has_side_effects=True, vmem_limit_bytes=56 * 1024 * 1024
        ),
    )(*operands)
    shape = jax.ShapeDtypeStruct((seq_rows, channels), jnp.bfloat16)
    return pl.pallas_call(
        tokens_kernel,
        out_shape=(shape, shape, shape),
        in_specs=[far, far],
        out_specs=(far, far, far),
        scratch_shapes=[
            pltpu.VMEM((3, channels, seq_rows), jnp.bfloat16),
            pltpu.VMEM((seq_rows, channels), jnp.bfloat16),
            pltpu.VMEM((3, seq_rows, channels), jnp.bfloat16),
            pltpu.SemaphoreType.DMA((channels // LANES + 1,)),
            pltpu.SemaphoreType.DMA((channels // LANES, 3)),
        ],
        compiler_params=pltpu.CompilerParams(vmem_limit_bytes=56 * 1024 * 1024),
    )(returned, grad_output)


def per_device(signal, gate_values, filter_taps, skip_gain, grad_output):
    groups = lax.axis_size("wide") * lax.axis_size("narrow")
    seq_rows, channels = signal.shape
    own = channels // groups
    fits = groups <= 32 and groups % 4 == 0 and seq_rows == LANES
    if fits and own >= CHUNK and own % CHUNK == 0 and channels % LANES == 0:
        return per_device_fused(signal, gate_values, filter_taps, skip_gain, grad_output)
    return per_device_plain(signal, gate_values, filter_taps, skip_gain, grad_output)


def solution(mesh):
    placed = (
        P(("parts", "wide", "narrow"), None),
        P(("parts", "wide", "narrow"), None),
        P(("wide", "narrow"), None),
        P(("wide", "narrow")),
        P(("parts", "wide", "narrow"), None),
    )
    return jax.shard_map(
        per_device,
        mesh=mesh,
        in_specs=placed,
        out_specs=(
            P(("parts", "wide", "narrow"), None),
            P(("parts", "wide", "narrow"), None),
            P(("parts", "wide", "narrow"), None),
        ),
        check_vma=False,
    )
```

```python
import functools
import math

import jax
import jax.numpy as jnp
import numpy as np
from jax import lax
from jax.experimental import pallas as pl
from jax.experimental.pallas import tpu as pltpu
from jax.sharding import PartitionSpec as P

precise = lax.Precision.HIGHEST


def angle_tables(left_count, right_count, period):
    left_index = jnp.arange(left_count, dtype=jnp.int32)
    right_index = jnp.arange(right_count, dtype=jnp.int32)
    phases = left_index[:, None] * right_index[None, :] % period
    angles = phases.astype(jnp.float32) * (2.0 * math.pi / period)
    return (jnp.cos(angles), jnp.sin(angles))


def spectral_tables(groups, seq_rows):
    full_span = 2 * groups * seq_rows
    outer_cos, outer_sin = angle_tables(2 * groups, groups, 2 * groups)
    twist_cos, twist_sin = angle_tables(2 * groups, seq_rows, full_span)
    inner_cos, inner_sin = angle_tables(seq_rows, seq_rows, seq_rows)
    return (outer_cos, outer_sin, twist_cos, twist_sin, inner_cos, inner_sin, full_span)


def transform(field, tables):
    outer_cos, outer_sin, twist_cos, twist_sin, inner_cos, inner_sin, full_span = tables
    first_real = jnp.einsum("ka,ucab->uckb", outer_cos, field, precision=precise)
    first_imag = -jnp.einsum("ka,ucab->uckb", outer_sin, field, precision=precise)
    turned_real = first_real * twist_cos + first_imag * twist_sin
    turned_imag = first_imag * twist_cos - first_real * twist_sin
    spec_real = jnp.einsum("uckb,bj->uckj", turned_real, inner_cos, precision=precise) + jnp.einsum(
        "uckb,bj->uckj", turned_imag, inner_sin, precision=precise
    )
    spec_imag = jnp.einsum("uckb,bj->uckj", turned_imag, inner_cos, precision=precise) - jnp.einsum(
        "uckb,bj->uckj", turned_real, inner_sin, precision=precise
    )
    return (spec_real, spec_imag)


def untwist(spec_real, spec_imag, tables):
    outer_cos, outer_sin, twist_cos, twist_sin, inner_cos, inner_sin, full_span = tables
    back_real = jnp.einsum("uckj,bj->uckb", spec_real, inner_cos, precision=precise) - jnp.einsum(
        "uckj,bj->uckb", spec_imag, inner_sin, precision=precise
    )
    back_imag = jnp.einsum("uckj,bj->uckb", spec_imag, inner_cos, precision=precise) + jnp.einsum(
        "uckj,bj->uckb", spec_real, inner_sin, precision=precise
    )
    turned_real = back_real * twist_cos - back_imag * twist_sin
    turned_imag = back_imag * twist_cos + back_real * twist_sin
    return (turned_real, turned_imag)


def inverse_real(spec_real, spec_imag, tables):
    outer_cos, outer_sin = (tables[0], tables[1])
    factor = 1.0 / tables[6]
    turned_real, turned_imag = untwist(spec_real, spec_imag, tables)
    out_real = jnp.einsum("ka,uckb->ucab", outer_cos, turned_real, precision=precise) - jnp.einsum(
        "ka,uckb->ucab", outer_sin, turned_imag, precision=precise
    )
    return out_real * factor


def to_channels(stacked, wide_count, narrow_count):
    stack_count, channels, seq_rows = stacked.shape
    groups = wide_count * narrow_count
    own_channels = channels // groups
    arrived = lax.all_to_all(stacked, ("wide", "narrow"), split_axis=1, concat_axis=2, tiled=True)
    return arrived.reshape(stack_count, own_channels, groups, seq_rows)


def to_sequence(field):
    stack_count, own_channels, groups, seq_rows = field.shape
    flat_field = field.reshape(stack_count, own_channels, groups * seq_rows)
    arrived = lax.all_to_all(
        flat_field, ("wide", "narrow"), split_axis=2, concat_axis=1, tiled=True
    )
    return arrived


def backward_channels(
    inner_chan,
    inner_real,
    inner_imag,
    signal_real,
    signal_imag,
    taps_real,
    taps_imag,
    skip_gain,
    tables,
    total_rows,
):
    taps_side_real = inner_real * taps_real + inner_imag * taps_imag
    taps_side_imag = inner_imag * taps_real - inner_real * taps_imag
    signal_side_real = inner_real * signal_real + inner_imag * signal_imag
    signal_side_imag = inner_imag * signal_real - inner_real * signal_imag
    back_taps = inverse_real(taps_side_real, taps_side_imag, tables)
    back_signal = inverse_real(signal_side_real, signal_side_imag, tables)
    signal_chan = (back_taps[0] + skip_gain[:, None, None] * inner_chan[0]).astype(jnp.bfloat16)
    filter_chan = (back_signal[0] * (1.0 / math.sqrt(total_rows))).astype(jnp.bfloat16)
    return (signal_chan, filter_chan)


def per_device_plain(signal, gate_values, filter_taps, skip_gain, grad_output):
    wide_count = lax.axis_size("wide")
    narrow_count = lax.axis_size("narrow")
    groups = wide_count * narrow_count
    seq_rows = signal.shape[0]
    total_rows = groups * seq_rows
    tables = spectral_tables(groups, seq_rows)
    grad_vals = grad_output.astype(jnp.float32)
    paired = jnp.stack([jnp.transpose(signal), jnp.transpose(filter_taps)])
    spread_pair = to_channels(paired, wide_count, narrow_count).astype(jnp.float32)
    pair_real, pair_imag = transform(spread_pair, tables)
    signal_real, signal_imag = (pair_real[0:1], pair_imag[0:1])
    taps_real, taps_imag = (pair_real[1:2], pair_imag[1:2])
    conv_real = signal_real * taps_real - signal_imag * taps_imag
    conv_imag = signal_real * taps_imag + signal_imag * taps_real
    convolved = inverse_real(conv_real, conv_imag, tables)[0]
    mixed_chan = (convolved + skip_gain[:, None, None] * spread_pair[0]).astype(jnp.bfloat16)
    mixed_rows = jnp.transpose(to_sequence(mixed_chan[None])[0])
    gate_grad = (grad_vals * mixed_rows.astype(jnp.float32)).astype(jnp.bfloat16)
    inner_grad = (grad_vals * gate_values.astype(jnp.float32)).astype(jnp.bfloat16)
    inner_chan = to_channels(jnp.transpose(inner_grad)[None], wide_count, narrow_count).astype(
        jnp.float32
    )
    inner_real, inner_imag = transform(inner_chan, tables)
    signal_chan, filter_chan = backward_channels(
        inner_chan,
        inner_real,
        inner_imag,
        signal_real,
        signal_imag,
        taps_real,
        taps_imag,
        skip_gain,
        tables,
        total_rows,
    )
    returned = to_sequence(jnp.stack([signal_chan, filter_chan]))
    signal_grad = jnp.transpose(returned[0])
    filter_grad = jnp.transpose(returned[1])
    return (signal_grad, gate_grad, filter_grad)


LANES = 128
CHUNK = 16
MESH = pl.DeviceIdType.MESH


def fused_tables(groups, seq_rows):
    span = 2 * groups * seq_rows
    kept = np.arange(groups + 1)[:, None]
    turn = 2.0 * np.pi * (kept * np.arange(seq_rows)[None, :]) / span
    weight = np.where((kept == 0) | (kept == groups), 1.0, 2.0) / span
    twist = np.stack([np.cos(turn), np.sin(turn), weight * np.cos(turn), weight * np.sin(turn)])
    index = np.arange(seq_rows)
    angle = 2.0 * np.pi * (index[:, None] * index[None, :] % seq_rows) / seq_rows
    cos, sin = np.cos(angle), np.sin(angle)
    ahead = np.block([[cos, -sin], [sin, cos]]).astype(np.float32)
    both = []
    for table in (ahead, ahead.T):
        high = table.astype(jnp.bfloat16)
        both += [high, (table - high.astype(np.float32)).astype(jnp.bfloat16)]
    return twist.astype(np.float32), np.stack(both)


def weighted_sum(pairs):
    by_size = {}
    for coefficient, array in pairs:
        if abs(coefficient) > 1e-9:
            key = round(abs(coefficient), 9)
            by_size.setdefault(key, (abs(coefficient), []))[1].append((coefficient > 0, array))
    total = None
    for size, members in by_size.values():
        members = sorted(members, key=lambda member: not member[0])
        positive = members[0][0]
        partial = members[0][1]
        for sign, array in members[1:]:
            partial = partial + array if sign == positive else partial - array
        factor = 1.0 if abs(size - 1.0) < 1e-9 else size
        if factor != 1.0:
            partial = partial * np.float32(factor)
        if total is None:
            total = partial if positive else -partial
        else:
            total = total + partial if positive else total - partial
    return total


def add(left, right):
    if left is None or right is None:
        return right if left is None else left
    return left + right


def sub(left, right):
    if left is None:
        return None if right is None else -right
    return left if right is None else left - right


def outer_forward(x):
    groups = len(x)
    half = groups // 2
    unit = math.pi / groups
    plus = {a: x[a] + x[groups - a] for a in range(1, half)}
    minus = {a: x[a] - x[groups - a] for a in range(1, half)}
    real, imag = [None] * (groups + 1), [None] * (groups + 1)
    for k in range(half + 1):
        even = k % 2 == 0
        cos_side, sin_side = (plus, minus) if even else (minus, plus)
        cos_parts, sin_parts = [[(1.0, x[0])], []], [[], []]
        cos_parts[half % 2].append((math.cos(unit * k * half), x[half]))
        sin_parts[half % 2].append((math.sin(unit * k * half), x[half]))
        for a in range(1, half):
            cos_parts[a % 2].append((math.cos(unit * k * a), cos_side[a]))
            sin_parts[a % 2].append((math.sin(unit * k * a), sin_side[a]))
        cos_even, cos_odd = weighted_sum(cos_parts[0]), weighted_sum(cos_parts[1])
        sin_even, sin_odd = weighted_sum(sin_parts[0]), weighted_sum(sin_parts[1])
        real[k] = add(cos_even, cos_odd)
        imag[k] = sub(sub(None, sin_even), sin_odd)
        real[groups - k] = sub(cos_even, cos_odd)
        if k < half:
            imag[groups - k] = sub(sin_even, sin_odd)
    zero = jnp.zeros_like(x[0])
    return [zero if v is None else v for v in real], [zero if v is None else v for v in imag]


def outer_inverse(real, imag):
    groups = len(real) - 1
    half = groups // 2
    unit = math.pi / groups
    out = [None] * groups
    for a_parity in (0, 1):
        cos_side, sin_side = {}, {}
        for k in range(1, half):
            if a_parity == 0:
                cos_side[k] = real[k] + real[groups - k]
                sin_side[k] = imag[k] - imag[groups - k]
            else:
                cos_side[k] = real[k] - real[groups - k]
                sin_side[k] = imag[k] + imag[groups - k]
        ends = real[0] + real[groups] if a_parity == 0 else real[0] - real[groups]
        for a in range(a_parity, half + 1, 2):
            cos_parts, sin_parts = [[(1.0, ends)], []], [[], []]
            cos_parts[half % 2].append((math.cos(unit * half * a), real[half]))
            sin_parts[half % 2].append((math.sin(unit * half * a), imag[half]))
            for k in range(1, half):
                cos_parts[k % 2].append((math.cos(unit * k * a), cos_side[k]))
                sin_parts[k % 2].append((math.sin(unit * k * a), sin_side[k]))
            cos_even, cos_odd = weighted_sum(cos_parts[0]), weighted_sum(cos_parts[1])
            sin_even, sin_odd = weighted_sum(sin_parts[0]), weighted_sum(sin_parts[1])
            out[a] = sub(sub(add(cos_even, cos_odd), sin_even), sin_odd)
            if 0 < a < half:
                out[groups - a] = sub(add(sub(cos_even, cos_odd), sin_even), sin_odd)
    return out


def split(value):
    high = value.astype(jnp.bfloat16)
    return high, (value - high.astype(jnp.float32)).astype(jnp.bfloat16)


def fused_kernel(
    groups,
    narrow_count,
    total_rows,
    signal_hbm,
    gate_hbm,
    taps_hbm,
    skip_hbm,
    grad_hbm,
    twist_hbm,
    inner_hbm,
    returned,
    signal_ref,
    gate_ref,
    taps_ref,
    skip_ref,
    grad_ref,
    twist_ref,
    inner_ref,
    outgoing,
    arrived,
    results,
    high_ref,
    low_ref,
    spec_ref,
    out_send,
    out_recv,
    back_send,
    back_recv,
    pass_send,
    pass_recv,
    local_sem,
    load_sem,
):
    seq_rows, channels = signal_ref.shape
    own = channels // groups
    chunks = own // CHUNK
    part = lax.axis_index("parts")
    me = lax.axis_index("wide") * narrow_count + lax.axis_index("narrow")
    twin = (1 - part, me // narrow_count, me % narrow_count)

    def device(index):
        return (part, index // narrow_count, index % narrow_count)

    barrier = pltpu.get_barrier_semaphore()
    pairs = [
        (signal_hbm, signal_ref),
        (taps_hbm, taps_ref),
        (grad_hbm, grad_ref),
        (gate_hbm, gate_ref),
        (skip_hbm, skip_ref),
        (twist_hbm, twist_ref),
        (inner_hbm, inner_ref),
    ]
    loads = [
        pltpu.make_async_copy(far, near, load_sem.at[i]) for i, (far, near) in enumerate(pairs)
    ]
    for load in loads:
        load.start()

    def greet(step, carry):
        pl.semaphore_signal(
            barrier, inc=1, device_id=device((me + step) % groups), device_id_type=MESH
        )
        return carry

    lax.fori_loop(1, groups, greet, 0)
    pl.semaphore_signal(barrier, inc=1, device_id=twin, device_id_type=MESH)

    def rows_of(index, chunk):
        return pl.ds(pl.multiple_of(index * own + chunk * CHUNK, CHUNK), CHUNK)

    def chunk_rows(chunk):
        return pl.ds(pl.multiple_of(chunk * CHUNK, CHUNK), CHUNK)

    def own_rows(index):
        return pl.ds(pl.multiple_of(index * own, CHUNK), own)

    def spread_whole(u, step):
        other = (me + step) % groups
        return pltpu.make_async_remote_copy(
            src_ref=outgoing.at[u, own_rows(other), :],
            dst_ref=arrived.at[me, u],
            send_sem=out_send.at[u, step],
            recv_sem=out_recv.at[u, step],
            device_id=device(other),
            device_id_type=MESH,
        )

    def spread_inner(chunk, step):
        other = (me + step) % groups
        return pltpu.make_async_remote_copy(
            src_ref=outgoing.at[2, rows_of(other, chunk), :],
            dst_ref=arrived.at[me, 2, chunk_rows(chunk), :],
            send_sem=out_send.at[2 + chunk, step],
            recv_sem=out_recv.at[2 + chunk, step],
            device_id=device(other),
            device_id_type=MESH,
        )

    def pass_on(source):
        return pltpu.make_async_remote_copy(
            src_ref=arrived.at[source, 1],
            dst_ref=arrived.at[source, 1],
            send_sem=pass_send.at[source],
            recv_sem=pass_recv.at[source],
            device_id=twin,
            device_id_type=MESH,
        )

    def for_others(action):
        def body(step, carry):
            action(step)
            return carry

        lax.fori_loop(1, groups, body, 0)

    def for_sources(parity, action):
        def body(i, carry):
            source = 2 * i + parity

            @pl.when(source != me)
            def _():
                action(source)

            return carry

        lax.fori_loop(0, groups // 2, body, 0)

    def bring(chunk, step):
        other = (me + step) % groups
        return pltpu.make_async_remote_copy(
            src_ref=results.at[other, :, chunk_rows(chunk), :],
            dst_ref=returned.at[:, rows_of(me, chunk), :],
            send_sem=back_send.at[chunk, step],
            recv_sem=back_recv.at[chunk, step],
            device_id=device(other),
            device_id_type=MESH,
        )

    spans = [slice(first, first + LANES) for first in range(0, channels, LANES)]
    loads[0].wait()
    for columns in spans:
        outgoing[0, columns, :] = signal_ref[:, columns].T
    pl.semaphore_wait(barrier, groups)
    for_others(lambda step: spread_whole(0, step).start())
    loads[1].wait()
    for columns in spans:
        outgoing[1, columns, :] = taps_ref[:, columns].T

    @pl.when(me % 2 == part)
    def _():
        for_others(lambda step: spread_whole(1, step).start())

    loads[2].wait()
    loads[3].wait()
    for columns in spans:
        grad_vals = grad_ref[:, columns].astype(jnp.float32)
        inner = (grad_vals * gate_ref[:, columns].astype(jnp.float32)).astype(jnp.bfloat16)
        outgoing[2, columns, :] = inner.T
    for chunk in range(chunks):
        for_others(lambda step, chunk=chunk: spread_inner(chunk, step).start())
    keep = pltpu.make_async_copy(
        outgoing.at[:, pl.ds(pl.multiple_of(me * own, CHUNK), own), :],
        arrived.at[me],
        local_sem,
    )
    keep.start()

    for load in loads[4:]:
        load.wait()
    lane = lax.broadcasted_iota(jnp.int32, (own, own), 1)
    row = lax.broadcasted_iota(jnp.int32, (own, own), 0)
    gain_all = jnp.sum(
        jnp.where(lane == row, jnp.broadcast_to(skip_ref[...], (own, own)), 0.0),
        axis=1,
        keepdims=True,
    )
    keep.wait()

    def take_taps(source):
        spread_whole(1, (me - source + groups) % groups).wait_recv()
        pass_on(source).start()

    for_sources(part, take_taps)
    for_others(lambda step: spread_whole(0, step).wait_recv())
    for_sources(1 - part, lambda source: pass_on(source).wait_recv())

    kept = groups + 1
    size = kept * 3 * CHUNK

    def inner_transform(which):
        high = high_ref[...].reshape(size, 2 * seq_rows)
        low = low_ref[...].reshape(size, 2 * seq_rows)
        table_high, table_low = inner_ref[which], inner_ref[which + 1]
        dot = functools.partial(jnp.dot, preferred_element_type=jnp.float32)
        total = dot(high, table_high) + dot(high, table_low) + dot(low, table_high)
        spec_ref[...] = total.reshape(kept, 3, CHUNK, 2 * seq_rows)

    def store_pair(k, u, real, imag):
        real_high, real_low = split(real)
        imag_high, imag_low = split(imag)
        high_ref[k, u, :, :seq_rows] = real_high
        high_ref[k, u, :, seq_rows:] = imag_high
        low_ref[k, u, :, :seq_rows] = real_low
        low_ref[k, u, :, seq_rows:] = imag_low

    for chunk in range(chunks):
        rows = slice(chunk * CHUNK, (chunk + 1) * CHUNK)
        for_others(lambda step, chunk=chunk: spread_inner(chunk, step).wait_recv())

        def ahead(u, carry, rows=rows):
            blocks = [arrived[a, u, rows, :].astype(jnp.float32) for a in range(groups)]
            real, imag = outer_forward(blocks)
            for k in range(kept):
                cos, sin = twist_ref[0, k : k + 1, :], twist_ref[1, k : k + 1, :]
                store_pair(
                    k, u, real[k] * cos + imag[k] * sin, imag[k] * cos - real[k] * sin
                )
            return carry

        lax.fori_loop(0, 3, ahead, 0)
        inner_transform(0)

        def multiply(k, carry):
            parts = [
                (spec_ref[k, u, :, :seq_rows], spec_ref[k, u, :, seq_rows:]) for u in range(3)
            ]
            (s_re, s_im), (t_re, t_im), (i_re, i_im) = parts
            store_pair(k, 0, s_re * t_re - s_im * t_im, s_re * t_im + s_im * t_re)
            store_pair(k, 1, i_re * t_re + i_im * t_im, i_im * t_re - i_re * t_im)
            store_pair(k, 2, i_re * s_re + i_im * s_im, i_im * s_re - i_re * s_im)
            return carry

        lax.fori_loop(0, kept, multiply, 0)
        inner_transform(2)

        gain = gain_all[rows, :]

        def back(u, carry, rows=rows, gain=gain):
            real, imag = [], []
            for k in range(kept):
                re, im = spec_ref[k, u, :, :seq_rows], spec_ref[k, u, :, seq_rows:]
                cos, sin = twist_ref[2, k : k + 1, :], twist_ref[3, k : k + 1, :]
                real.append(re * cos - im * sin)
                imag.append(im * cos + re * sin)
            for a, block in enumerate(outer_inverse(real, imag)):
                skipped = arrived[a, 2 * u, rows, :].astype(jnp.float32)
                results[a, u, rows, :] = (block + gain * skipped).astype(jnp.bfloat16)
            return carry

        lax.fori_loop(0, 2, back, 0)
        real, imag = [], []
        for k in range(kept):
            re, im = spec_ref[k, 2, :, :seq_rows], spec_ref[k, 2, :, seq_rows:]
            cos, sin = twist_ref[2, k : k + 1, :], twist_ref[3, k : k + 1, :]
            real.append(re * cos - im * sin)
            imag.append(im * cos + re * sin)
        for a, block in enumerate(outer_inverse(real, imag)):
            scaled = block * np.float32(1.0 / math.sqrt(total_rows))
            results[a, 2, rows, :] = scaled.astype(jnp.bfloat16)

        def start_back(step, carry, chunk=chunk):
            bring(chunk, step).start()
            return carry

        lax.fori_loop(1, groups, start_back, 0)

    mine = pltpu.make_async_copy(
        results.at[me],
        returned.at[:, pl.ds(pl.multiple_of(me * own, CHUNK), own), :],
        local_sem,
    )
    mine.start()
    mine.wait()
    for chunk in range(chunks):

        def finish(step, carry, chunk=chunk):
            bring(chunk, step).wait_recv()
            return carry

        lax.fori_loop(1, groups, finish, 0)

    for_others(lambda step: spread_whole(0, step).wait_send())

    @pl.when(me % 2 == part)
    def _():
        for_others(lambda step: spread_whole(1, step).wait_send())

    for_sources(part, lambda source: pass_on(source).wait_send())
    for chunk in range(chunks):
        for_others(lambda step, chunk=chunk: spread_inner(chunk, step).wait_send())
        for_others(lambda step, chunk=chunk: bring(chunk, step).wait_send())


def tokens_kernel(
    returned_hbm,
    grad_hbm,
    signal_out,
    gate_out,
    filter_out,
    returned,
    grad_ref,
    staged,
    load_sems,
    sems,
):
    outs = (signal_out, gate_out, filter_out)
    copies = []
    spans = [slice(first, first + LANES) for first in range(0, grad_ref.shape[1], LANES)]
    grad_load = pltpu.make_async_copy(grad_hbm, grad_ref, load_sems.at[len(spans)])
    grad_load.start()
    loads = [
        pltpu.make_async_copy(
            returned_hbm.at[:, columns, :], returned.at[:, columns, :], load_sems.at[block]
        )
        for block, columns in enumerate(spans)
    ]
    for load in loads:
        load.start()
    grad_load.wait()
    for block, columns in enumerate(spans):
        loads[block].wait()
        mixed = returned[0, columns, :].T.astype(jnp.float32)
        staged[0, :, columns] = returned[1, columns, :].T
        staged[1, :, columns] = (grad_ref[:, columns].astype(jnp.float32) * mixed).astype(
            jnp.bfloat16
        )
        staged[2, :, columns] = returned[2, columns, :].T
        for u in range(3):
            copies.append(
                pltpu.make_async_copy(
                    staged.at[u, :, columns], outs[u].at[:, columns], sems.at[block, u]
                )
            )
            copies[-1].start()
    for copy in copies:
        copy.wait()


def per_device_fused(signal, gate_values, filter_taps, skip_gain, grad_output):
    narrow_count = lax.axis_size("narrow")
    groups = lax.axis_size("wide") * narrow_count
    seq_rows, channels = signal.shape
    own = channels // groups
    chunks = own // CHUNK
    twist, inner = fused_tables(groups, seq_rows)
    far = pl.BlockSpec(memory_space=pl.ANY)
    rows = (groups + 1, 3, CHUNK, 2 * seq_rows)
    operands = (
        signal,
        gate_values,
        filter_taps,
        skip_gain[None, :],
        grad_output,
        jnp.asarray(twist),
        jnp.asarray(inner),
    )
    returned = pl.pallas_call(
        functools.partial(fused_kernel, groups, narrow_count, groups * seq_rows),
        out_shape=jax.ShapeDtypeStruct((3, channels, seq_rows), jnp.bfloat16),
        in_specs=[far] * len(operands),
        out_specs=far,
        scratch_shapes=[
            *[pltpu.VMEM(operand.shape, operand.dtype) for operand in operands],
            pltpu.VMEM((3, channels, seq_rows), jnp.bfloat16),
            pltpu.VMEM((groups, 3, own, seq_rows), jnp.bfloat16),
            pltpu.VMEM((groups, 3, own, seq_rows), jnp.bfloat16),
            pltpu.VMEM(rows, jnp.bfloat16),
            pltpu.VMEM(rows, jnp.bfloat16),
            pltpu.VMEM(rows, jnp.float32),
            pltpu.SemaphoreType.DMA((2 + chunks, groups)),
            pltpu.SemaphoreType.DMA((2 + chunks, groups)),
            pltpu.SemaphoreType.DMA((chunks, groups)),
            pltpu.SemaphoreType.DMA((chunks, groups)),
            pltpu.SemaphoreType.DMA((groups,)),
            pltpu.SemaphoreType.DMA((groups,)),
            pltpu.SemaphoreType.DMA,
            pltpu.SemaphoreType.DMA((len(operands),)),
        ],
        compiler_params=pltpu.CompilerParams(
            collective_id=0, has_side_effects=True, vmem_limit_bytes=56 * 1024 * 1024
        ),
    )(*operands)
    shape = jax.ShapeDtypeStruct((seq_rows, channels), jnp.bfloat16)
    return pl.pallas_call(
        tokens_kernel,
        out_shape=(shape, shape, shape),
        in_specs=[far, far],
        out_specs=(far, far, far),
        scratch_shapes=[
            pltpu.VMEM((3, channels, seq_rows), jnp.bfloat16),
            pltpu.VMEM((seq_rows, channels), jnp.bfloat16),
            pltpu.VMEM((3, seq_rows, channels), jnp.bfloat16),
            pltpu.SemaphoreType.DMA((channels // LANES + 1,)),
            pltpu.SemaphoreType.DMA((channels // LANES, 3)),
        ],
        compiler_params=pltpu.CompilerParams(vmem_limit_bytes=56 * 1024 * 1024),
    )(returned, grad_output)


def per_device(signal, gate_values, filter_taps, skip_gain, grad_output):
    groups = lax.axis_size("wide") * lax.axis_size("narrow")
    seq_rows, channels = signal.shape
    own = channels // groups
    fits = groups <= 32 and groups % 4 == 0 and seq_rows == LANES
    fits = fits and lax.axis_size("parts") == 2
    if fits and own >= CHUNK and own % CHUNK == 0 and channels % LANES == 0:
        return per_device_fused(signal, gate_values, filter_taps, skip_gain, grad_output)
    return per_device_plain(signal, gate_values, filter_taps, skip_gain, grad_output)


def solution(mesh):
    placed = (
        P(("parts", "wide", "narrow"), None),
        P(("parts", "wide", "narrow"), None),
        P(("wide", "narrow"), None),
        P(("wide", "narrow")),
        P(("parts", "wide", "narrow"), None),
    )
    return jax.shard_map(
        per_device,
        mesh=mesh,
        in_specs=placed,
        out_specs=(
            P(("parts", "wide", "narrow"), None),
            P(("parts", "wide", "narrow"), None),
            P(("parts", "wide", "narrow"), None),
        ),
        check_vma=False,
    )
```

```python
import functools
import math

import jax
import jax.numpy as jnp
import numpy as np
from jax import lax
from jax.experimental import pallas as pl
from jax.experimental.pallas import tpu as pltpu
from jax.sharding import PartitionSpec as P

precise = lax.Precision.HIGHEST


def angle_tables(left_count, right_count, period):
    left_index = jnp.arange(left_count, dtype=jnp.int32)
    right_index = jnp.arange(right_count, dtype=jnp.int32)
    phases = left_index[:, None] * right_index[None, :] % period
    angles = phases.astype(jnp.float32) * (2.0 * math.pi / period)
    return (jnp.cos(angles), jnp.sin(angles))


def spectral_tables(groups, seq_rows):
    full_span = 2 * groups * seq_rows
    outer_cos, outer_sin = angle_tables(2 * groups, groups, 2 * groups)
    twist_cos, twist_sin = angle_tables(2 * groups, seq_rows, full_span)
    inner_cos, inner_sin = angle_tables(seq_rows, seq_rows, seq_rows)
    return (outer_cos, outer_sin, twist_cos, twist_sin, inner_cos, inner_sin, full_span)


def transform(field, tables):
    outer_cos, outer_sin, twist_cos, twist_sin, inner_cos, inner_sin, full_span = tables
    first_real = jnp.einsum("ka,ucab->uckb", outer_cos, field, precision=precise)
    first_imag = -jnp.einsum("ka,ucab->uckb", outer_sin, field, precision=precise)
    turned_real = first_real * twist_cos + first_imag * twist_sin
    turned_imag = first_imag * twist_cos - first_real * twist_sin
    spec_real = jnp.einsum("uckb,bj->uckj", turned_real, inner_cos, precision=precise) + jnp.einsum(
        "uckb,bj->uckj", turned_imag, inner_sin, precision=precise
    )
    spec_imag = jnp.einsum("uckb,bj->uckj", turned_imag, inner_cos, precision=precise) - jnp.einsum(
        "uckb,bj->uckj", turned_real, inner_sin, precision=precise
    )
    return (spec_real, spec_imag)


def untwist(spec_real, spec_imag, tables):
    outer_cos, outer_sin, twist_cos, twist_sin, inner_cos, inner_sin, full_span = tables
    back_real = jnp.einsum("uckj,bj->uckb", spec_real, inner_cos, precision=precise) - jnp.einsum(
        "uckj,bj->uckb", spec_imag, inner_sin, precision=precise
    )
    back_imag = jnp.einsum("uckj,bj->uckb", spec_imag, inner_cos, precision=precise) + jnp.einsum(
        "uckj,bj->uckb", spec_real, inner_sin, precision=precise
    )
    turned_real = back_real * twist_cos - back_imag * twist_sin
    turned_imag = back_imag * twist_cos + back_real * twist_sin
    return (turned_real, turned_imag)


def inverse_real(spec_real, spec_imag, tables):
    outer_cos, outer_sin = (tables[0], tables[1])
    factor = 1.0 / tables[6]
    turned_real, turned_imag = untwist(spec_real, spec_imag, tables)
    out_real = jnp.einsum("ka,uckb->ucab", outer_cos, turned_real, precision=precise) - jnp.einsum(
        "ka,uckb->ucab", outer_sin, turned_imag, precision=precise
    )
    return out_real * factor


def to_channels(stacked, wide_count, narrow_count):
    stack_count, channels, seq_rows = stacked.shape
    groups = wide_count * narrow_count
    own_channels = channels // groups
    arrived = lax.all_to_all(stacked, ("wide", "narrow"), split_axis=1, concat_axis=2, tiled=True)
    return arrived.reshape(stack_count, own_channels, groups, seq_rows)


def to_sequence(field):
    stack_count, own_channels, groups, seq_rows = field.shape
    flat_field = field.reshape(stack_count, own_channels, groups * seq_rows)
    arrived = lax.all_to_all(
        flat_field, ("wide", "narrow"), split_axis=2, concat_axis=1, tiled=True
    )
    return arrived


def backward_channels(
    inner_chan,
    inner_real,
    inner_imag,
    signal_real,
    signal_imag,
    taps_real,
    taps_imag,
    skip_gain,
    tables,
    total_rows,
):
    taps_side_real = inner_real * taps_real + inner_imag * taps_imag
    taps_side_imag = inner_imag * taps_real - inner_real * taps_imag
    signal_side_real = inner_real * signal_real + inner_imag * signal_imag
    signal_side_imag = inner_imag * signal_real - inner_real * signal_imag
    back_taps = inverse_real(taps_side_real, taps_side_imag, tables)
    back_signal = inverse_real(signal_side_real, signal_side_imag, tables)
    signal_chan = (back_taps[0] + skip_gain[:, None, None] * inner_chan[0]).astype(jnp.bfloat16)
    filter_chan = (back_signal[0] * (1.0 / math.sqrt(total_rows))).astype(jnp.bfloat16)
    return (signal_chan, filter_chan)


def per_device_plain(signal, gate_values, filter_taps, skip_gain, grad_output):
    wide_count = lax.axis_size("wide")
    narrow_count = lax.axis_size("narrow")
    groups = wide_count * narrow_count
    seq_rows = signal.shape[0]
    total_rows = groups * seq_rows
    tables = spectral_tables(groups, seq_rows)
    grad_vals = grad_output.astype(jnp.float32)
    paired = jnp.stack([jnp.transpose(signal), jnp.transpose(filter_taps)])
    spread_pair = to_channels(paired, wide_count, narrow_count).astype(jnp.float32)
    pair_real, pair_imag = transform(spread_pair, tables)
    signal_real, signal_imag = (pair_real[0:1], pair_imag[0:1])
    taps_real, taps_imag = (pair_real[1:2], pair_imag[1:2])
    conv_real = signal_real * taps_real - signal_imag * taps_imag
    conv_imag = signal_real * taps_imag + signal_imag * taps_real
    convolved = inverse_real(conv_real, conv_imag, tables)[0]
    mixed_chan = (convolved + skip_gain[:, None, None] * spread_pair[0]).astype(jnp.bfloat16)
    mixed_rows = jnp.transpose(to_sequence(mixed_chan[None])[0])
    gate_grad = (grad_vals * mixed_rows.astype(jnp.float32)).astype(jnp.bfloat16)
    inner_grad = (grad_vals * gate_values.astype(jnp.float32)).astype(jnp.bfloat16)
    inner_chan = to_channels(jnp.transpose(inner_grad)[None], wide_count, narrow_count).astype(
        jnp.float32
    )
    inner_real, inner_imag = transform(inner_chan, tables)
    signal_chan, filter_chan = backward_channels(
        inner_chan,
        inner_real,
        inner_imag,
        signal_real,
        signal_imag,
        taps_real,
        taps_imag,
        skip_gain,
        tables,
        total_rows,
    )
    returned = to_sequence(jnp.stack([signal_chan, filter_chan]))
    signal_grad = jnp.transpose(returned[0])
    filter_grad = jnp.transpose(returned[1])
    return (signal_grad, gate_grad, filter_grad)


LANES = 128
CHUNK = 16
MESH = pl.DeviceIdType.MESH


def fused_tables(groups, seq_rows):
    span = 2 * groups * seq_rows
    kept = np.arange(groups + 1)[:, None]
    turn = 2.0 * np.pi * (kept * np.arange(seq_rows)[None, :]) / span
    weight = np.where((kept == 0) | (kept == groups), 1.0, 2.0) / span
    twist = np.stack([np.cos(turn), np.sin(turn), weight * np.cos(turn), weight * np.sin(turn)])
    index = np.arange(seq_rows)
    angle = 2.0 * np.pi * (index[:, None] * index[None, :] % seq_rows) / seq_rows
    cos, sin = np.cos(angle), np.sin(angle)
    ahead = np.block([[cos, -sin], [sin, cos]]).astype(np.float32)
    both = []
    for table in (ahead, ahead.T):
        high = table.astype(jnp.bfloat16)
        both += [high, (table - high.astype(np.float32)).astype(jnp.bfloat16)]
    return twist.astype(np.float32), np.stack(both)


def weighted_sum(pairs):
    by_size = {}
    for coefficient, array in pairs:
        if abs(coefficient) > 1e-9:
            key = round(abs(coefficient), 9)
            by_size.setdefault(key, (abs(coefficient), []))[1].append((coefficient > 0, array))
    total = None
    for size, members in by_size.values():
        members = sorted(members, key=lambda member: not member[0])
        positive = members[0][0]
        partial = members[0][1]
        for sign, array in members[1:]:
            partial = partial + array if sign == positive else partial - array
        factor = 1.0 if abs(size - 1.0) < 1e-9 else size
        if factor != 1.0:
            partial = partial * np.float32(factor)
        if total is None:
            total = partial if positive else -partial
        else:
            total = total + partial if positive else total - partial
    return total


def add(left, right):
    if left is None or right is None:
        return right if left is None else left
    return left + right


def sub(left, right):
    if left is None:
        return None if right is None else -right
    return left if right is None else left - right


def outer_forward(x):
    groups = len(x)
    half = groups // 2
    unit = math.pi / groups
    plus = {a: x[a] + x[groups - a] for a in range(1, half)}
    minus = {a: x[a] - x[groups - a] for a in range(1, half)}
    real, imag = [None] * (groups + 1), [None] * (groups + 1)
    for k in range(half + 1):
        even = k % 2 == 0
        cos_side, sin_side = (plus, minus) if even else (minus, plus)
        cos_parts, sin_parts = [[(1.0, x[0])], []], [[], []]
        cos_parts[half % 2].append((math.cos(unit * k * half), x[half]))
        sin_parts[half % 2].append((math.sin(unit * k * half), x[half]))
        for a in range(1, half):
            cos_parts[a % 2].append((math.cos(unit * k * a), cos_side[a]))
            sin_parts[a % 2].append((math.sin(unit * k * a), sin_side[a]))
        cos_even, cos_odd = weighted_sum(cos_parts[0]), weighted_sum(cos_parts[1])
        sin_even, sin_odd = weighted_sum(sin_parts[0]), weighted_sum(sin_parts[1])
        real[k] = add(cos_even, cos_odd)
        imag[k] = sub(sub(None, sin_even), sin_odd)
        real[groups - k] = sub(cos_even, cos_odd)
        if k < half:
            imag[groups - k] = sub(sin_even, sin_odd)
    zero = jnp.zeros_like(x[0])
    return [zero if v is None else v for v in real], [zero if v is None else v for v in imag]


def outer_inverse(real, imag):
    groups = len(real) - 1
    half = groups // 2
    unit = math.pi / groups
    out = [None] * groups
    for a_parity in (0, 1):
        cos_side, sin_side = {}, {}
        for k in range(1, half):
            if a_parity == 0:
                cos_side[k] = real[k] + real[groups - k]
                sin_side[k] = imag[k] - imag[groups - k]
            else:
                cos_side[k] = real[k] - real[groups - k]
                sin_side[k] = imag[k] + imag[groups - k]
        ends = real[0] + real[groups] if a_parity == 0 else real[0] - real[groups]
        for a in range(a_parity, half + 1, 2):
            cos_parts, sin_parts = [[(1.0, ends)], []], [[], []]
            cos_parts[half % 2].append((math.cos(unit * half * a), real[half]))
            sin_parts[half % 2].append((math.sin(unit * half * a), imag[half]))
            for k in range(1, half):
                cos_parts[k % 2].append((math.cos(unit * k * a), cos_side[k]))
                sin_parts[k % 2].append((math.sin(unit * k * a), sin_side[k]))
            cos_even, cos_odd = weighted_sum(cos_parts[0]), weighted_sum(cos_parts[1])
            sin_even, sin_odd = weighted_sum(sin_parts[0]), weighted_sum(sin_parts[1])
            out[a] = sub(sub(add(cos_even, cos_odd), sin_even), sin_odd)
            if 0 < a < half:
                out[groups - a] = sub(add(sub(cos_even, cos_odd), sin_even), sin_odd)
    return out


def split(value):
    high = value.astype(jnp.bfloat16)
    return high, (value - high.astype(jnp.float32)).astype(jnp.bfloat16)


def fused_kernel(
    groups,
    narrow_count,
    total_rows,
    signal_hbm,
    gate_hbm,
    taps_hbm,
    skip_hbm,
    grad_hbm,
    twist_hbm,
    inner_hbm,
    returned,
    signal_ref,
    gate_ref,
    taps_ref,
    skip_ref,
    grad_ref,
    twist_ref,
    inner_ref,
    outgoing,
    arrived,
    results,
    high_ref,
    low_ref,
    spec_ref,
    out_send,
    out_recv,
    back_send,
    back_recv,
    pass_send,
    pass_recv,
    local_sem,
    load_sem,
):
    seq_rows, channels = signal_ref.shape
    own = channels // groups
    chunks = own // CHUNK
    part = lax.axis_index("parts")
    me = lax.axis_index("wide") * narrow_count + lax.axis_index("narrow")
    twin = (1 - part, me // narrow_count, me % narrow_count)

    def device(index):
        return (part, index // narrow_count, index % narrow_count)

    barrier = pltpu.get_barrier_semaphore()
    pairs = [
        (signal_hbm, signal_ref),
        (taps_hbm, taps_ref),
        (grad_hbm, grad_ref),
        (gate_hbm, gate_ref),
        (skip_hbm, skip_ref),
        (twist_hbm, twist_ref),
        (inner_hbm, inner_ref),
    ]
    loads = [
        pltpu.make_async_copy(far, near, load_sem.at[i]) for i, (far, near) in enumerate(pairs)
    ]
    for load in loads:
        load.start()

    def greet(step, carry):
        pl.semaphore_signal(
            barrier, inc=1, device_id=device((me + step) % groups), device_id_type=MESH
        )
        return carry

    lax.fori_loop(1, groups, greet, 0)
    pl.semaphore_signal(barrier, inc=1, device_id=twin, device_id_type=MESH)

    def rows_of(index, chunk):
        return pl.ds(pl.multiple_of(index * own + chunk * CHUNK, CHUNK), CHUNK)

    def chunk_rows(chunk):
        return pl.ds(pl.multiple_of(chunk * CHUNK, CHUNK), CHUNK)

    def own_rows(index):
        return pl.ds(pl.multiple_of(index * own, CHUNK), own)

    def spread_pair(chunk, step):
        other = (me + step) % groups
        return pltpu.make_async_remote_copy(
            src_ref=outgoing.at[0:2, rows_of(other, chunk), :],
            dst_ref=arrived.at[me, 0:2, chunk_rows(chunk), :],
            send_sem=out_send.at[chunk, step],
            recv_sem=out_recv.at[chunk, step],
            device_id=device(other),
            device_id_type=MESH,
        )

    def spread_taps(chunk, step):
        other = (me + step) % groups
        return pltpu.make_async_remote_copy(
            src_ref=outgoing.at[2, rows_of(other, chunk), :],
            dst_ref=arrived.at[me, 2, chunk_rows(chunk), :],
            send_sem=out_send.at[chunks + chunk, step],
            recv_sem=out_recv.at[chunks + chunk, step],
            device_id=device(other),
            device_id_type=MESH,
        )

    def pass_on(chunk, source):
        return pltpu.make_async_remote_copy(
            src_ref=arrived.at[source, 2, chunk_rows(chunk), :],
            dst_ref=arrived.at[source, 2, chunk_rows(chunk), :],
            send_sem=pass_send.at[chunk, source],
            recv_sem=pass_recv.at[chunk, source],
            device_id=twin,
            device_id_type=MESH,
        )

    def for_others(action):
        def body(step, carry):
            action(step)
            return carry

        lax.fori_loop(1, groups, body, 0)

    def for_sources(parity, action):
        def body(i, carry):
            source = 2 * i + parity

            @pl.when(source != me)
            def _():
                action(source)

            return carry

        lax.fori_loop(0, groups // 2, body, 0)

    def bring(chunk, step):
        other = (me + step) % groups
        return pltpu.make_async_remote_copy(
            src_ref=results.at[other, :, chunk_rows(chunk), :],
            dst_ref=returned.at[:, rows_of(me, chunk), :],
            send_sem=back_send.at[chunk, step],
            recv_sem=back_recv.at[chunk, step],
            device_id=device(other),
            device_id_type=MESH,
        )

    spans = [slice(first, first + LANES) for first in range(0, channels, LANES)]
    for load in loads[:4]:
        load.wait()
    for columns in spans:
        grad_vals = grad_ref[:, columns].astype(jnp.float32)
        inner = (grad_vals * gate_ref[:, columns].astype(jnp.float32)).astype(jnp.bfloat16)
        outgoing[0, columns, :] = signal_ref[:, columns].T
        outgoing[1, columns, :] = inner.T
        outgoing[2, columns, :] = taps_ref[:, columns].T
    pl.semaphore_wait(barrier, groups)
    for chunk in range(chunks):

        @pl.when(me % 2 == part)
        def _(chunk=chunk):
            for_others(lambda step: spread_taps(chunk, step).start())

        for_others(lambda step, chunk=chunk: spread_pair(chunk, step).start())
    keep = pltpu.make_async_copy(
        outgoing.at[:, pl.ds(pl.multiple_of(me * own, CHUNK), own), :],
        arrived.at[me],
        local_sem,
    )
    keep.start()

    for load in loads[4:]:
        load.wait()
    lane = lax.broadcasted_iota(jnp.int32, (own, own), 1)
    row = lax.broadcasted_iota(jnp.int32, (own, own), 0)
    gain_all = jnp.sum(
        jnp.where(lane == row, jnp.broadcast_to(skip_ref[...], (own, own)), 0.0),
        axis=1,
        keepdims=True,
    )
    keep.wait()

    def take_taps(chunk, source):
        spread_taps(chunk, (me - source + groups) % groups).wait_recv()
        pass_on(chunk, source).start()

    for_sources(part, functools.partial(take_taps, 0))

    kept = groups + 1
    size = kept * 3 * CHUNK

    def inner_transform(which):
        high = high_ref[...].reshape(size, 2 * seq_rows)
        low = low_ref[...].reshape(size, 2 * seq_rows)
        table_high, table_low = inner_ref[which], inner_ref[which + 1]
        dot = functools.partial(jnp.dot, preferred_element_type=jnp.float32)
        total = dot(high, table_high) + dot(high, table_low) + dot(low, table_high)
        spec_ref[...] = total.reshape(kept, 3, CHUNK, 2 * seq_rows)

    def store_pair(k, u, real, imag):
        real_high, real_low = split(real)
        imag_high, imag_low = split(imag)
        high_ref[k, u, :, :seq_rows] = real_high
        high_ref[k, u, :, seq_rows:] = imag_high
        low_ref[k, u, :, :seq_rows] = real_low
        low_ref[k, u, :, seq_rows:] = imag_low

    for chunk in range(chunks):
        rows = slice(chunk * CHUNK, (chunk + 1) * CHUNK)
        for_others(lambda step, chunk=chunk: spread_pair(chunk, step).wait_recv())
        for_sources(1 - part, lambda source, chunk=chunk: pass_on(chunk, source).wait_recv())

        def ahead(u, carry, rows=rows):
            blocks = [arrived[a, u, rows, :].astype(jnp.float32) for a in range(groups)]
            real, imag = outer_forward(blocks)
            for k in range(kept):
                cos, sin = twist_ref[0, k : k + 1, :], twist_ref[1, k : k + 1, :]
                store_pair(
                    k, u, real[k] * cos + imag[k] * sin, imag[k] * cos - real[k] * sin
                )
            return carry

        lax.fori_loop(0, 3, ahead, 0)
        inner_transform(0)

        def multiply(k, carry):
            parts = [
                (spec_ref[k, u, :, :seq_rows], spec_ref[k, u, :, seq_rows:]) for u in range(3)
            ]
            (s_re, s_im), (i_re, i_im), (t_re, t_im) = parts
            store_pair(k, 0, s_re * t_re - s_im * t_im, s_re * t_im + s_im * t_re)
            store_pair(k, 1, i_re * t_re + i_im * t_im, i_im * t_re - i_re * t_im)
            store_pair(k, 2, i_re * s_re + i_im * s_im, i_im * s_re - i_re * s_im)
            return carry

        lax.fori_loop(0, kept, multiply, 0)
        if chunk + 1 < chunks:
            for_sources(part, functools.partial(take_taps, chunk + 1))
        inner_transform(2)

        gain = gain_all[rows, :]

        def back(u, carry, rows=rows, gain=gain):
            real, imag = [], []
            for k in range(kept):
                re, im = spec_ref[k, u, :, :seq_rows], spec_ref[k, u, :, seq_rows:]
                cos, sin = twist_ref[2, k : k + 1, :], twist_ref[3, k : k + 1, :]
                real.append(re * cos - im * sin)
                imag.append(im * cos + re * sin)
            for a, block in enumerate(outer_inverse(real, imag)):
                skipped = arrived[a, u, rows, :].astype(jnp.float32)
                results[a, u, rows, :] = (block + gain * skipped).astype(jnp.bfloat16)
            return carry

        lax.fori_loop(0, 2, back, 0)
        real, imag = [], []
        for k in range(kept):
            re, im = spec_ref[k, 2, :, :seq_rows], spec_ref[k, 2, :, seq_rows:]
            cos, sin = twist_ref[2, k : k + 1, :], twist_ref[3, k : k + 1, :]
            real.append(re * cos - im * sin)
            imag.append(im * cos + re * sin)
        for a, block in enumerate(outer_inverse(real, imag)):
            scaled = block * np.float32(1.0 / math.sqrt(total_rows))
            results[a, 2, rows, :] = scaled.astype(jnp.bfloat16)

        def start_back(step, carry, chunk=chunk):
            bring(chunk, step).start()
            return carry

        lax.fori_loop(1, groups, start_back, 0)

    mine = pltpu.make_async_copy(
        results.at[me],
        returned.at[:, pl.ds(pl.multiple_of(me * own, CHUNK), own), :],
        local_sem,
    )
    mine.start()
    mine.wait()
    for chunk in range(chunks):

        def finish(step, carry, chunk=chunk):
            bring(chunk, step).wait_recv()
            return carry

        lax.fori_loop(1, groups, finish, 0)

    for chunk in range(chunks):
        for_others(lambda step, chunk=chunk: spread_pair(chunk, step).wait_send())

        @pl.when(me % 2 == part)
        def _(chunk=chunk):
            for_others(lambda step: spread_taps(chunk, step).wait_send())

        for_sources(part, lambda source, chunk=chunk: pass_on(chunk, source).wait_send())
        for_others(lambda step, chunk=chunk: bring(chunk, step).wait_send())


def tokens_kernel(
    returned_hbm,
    grad_hbm,
    signal_out,
    gate_out,
    filter_out,
    returned,
    grad_ref,
    staged,
    load_sems,
    sems,
):
    outs = (signal_out, gate_out, filter_out)
    copies = []
    spans = [slice(first, first + LANES) for first in range(0, grad_ref.shape[1], LANES)]
    grad_load = pltpu.make_async_copy(grad_hbm, grad_ref, load_sems.at[len(spans)])
    grad_load.start()
    loads = [
        pltpu.make_async_copy(
            returned_hbm.at[:, columns, :], returned.at[:, columns, :], load_sems.at[block]
        )
        for block, columns in enumerate(spans)
    ]
    for load in loads:
        load.start()
    grad_load.wait()
    for block, columns in enumerate(spans):
        loads[block].wait()
        mixed = returned[0, columns, :].T.astype(jnp.float32)
        staged[0, :, columns] = returned[1, columns, :].T
        staged[1, :, columns] = (grad_ref[:, columns].astype(jnp.float32) * mixed).astype(
            jnp.bfloat16
        )
        staged[2, :, columns] = returned[2, columns, :].T
        for u in range(3):
            copies.append(
                pltpu.make_async_copy(
                    staged.at[u, :, columns], outs[u].at[:, columns], sems.at[block, u]
                )
            )
            copies[-1].start()
    for copy in copies:
        copy.wait()


def per_device_fused(signal, gate_values, filter_taps, skip_gain, grad_output):
    narrow_count = lax.axis_size("narrow")
    groups = lax.axis_size("wide") * narrow_count
    seq_rows, channels = signal.shape
    own = channels // groups
    chunks = own // CHUNK
    twist, inner = fused_tables(groups, seq_rows)
    far = pl.BlockSpec(memory_space=pl.ANY)
    rows = (groups + 1, 3, CHUNK, 2 * seq_rows)
    operands = (
        signal,
        gate_values,
        filter_taps,
        skip_gain[None, :],
        grad_output,
        jnp.asarray(twist),
        jnp.asarray(inner),
    )
    returned = pl.pallas_call(
        functools.partial(fused_kernel, groups, narrow_count, groups * seq_rows),
        out_shape=jax.ShapeDtypeStruct((3, channels, seq_rows), jnp.bfloat16),
        in_specs=[far] * len(operands),
        out_specs=far,
        scratch_shapes=[
            *[pltpu.VMEM(operand.shape, operand.dtype) for operand in operands],
            pltpu.VMEM((3, channels, seq_rows), jnp.bfloat16),
            pltpu.VMEM((groups, 3, own, seq_rows), jnp.bfloat16),
            pltpu.VMEM((groups, 3, own, seq_rows), jnp.bfloat16),
            pltpu.VMEM(rows, jnp.bfloat16),
            pltpu.VMEM(rows, jnp.bfloat16),
            pltpu.VMEM(rows, jnp.float32),
            pltpu.SemaphoreType.DMA((2 * chunks, groups)),
            pltpu.SemaphoreType.DMA((2 * chunks, groups)),
            pltpu.SemaphoreType.DMA((chunks, groups)),
            pltpu.SemaphoreType.DMA((chunks, groups)),
            pltpu.SemaphoreType.DMA((chunks, groups)),
            pltpu.SemaphoreType.DMA((chunks, groups)),
            pltpu.SemaphoreType.DMA,
            pltpu.SemaphoreType.DMA((len(operands),)),
        ],
        compiler_params=pltpu.CompilerParams(
            collective_id=0, has_side_effects=True, vmem_limit_bytes=56 * 1024 * 1024
        ),
    )(*operands)
    shape = jax.ShapeDtypeStruct((seq_rows, channels), jnp.bfloat16)
    return pl.pallas_call(
        tokens_kernel,
        out_shape=(shape, shape, shape),
        in_specs=[far, far],
        out_specs=(far, far, far),
        scratch_shapes=[
            pltpu.VMEM((3, channels, seq_rows), jnp.bfloat16),
            pltpu.VMEM((seq_rows, channels), jnp.bfloat16),
            pltpu.VMEM((3, seq_rows, channels), jnp.bfloat16),
            pltpu.SemaphoreType.DMA((channels // LANES + 1,)),
            pltpu.SemaphoreType.DMA((channels // LANES, 3)),
        ],
        compiler_params=pltpu.CompilerParams(vmem_limit_bytes=56 * 1024 * 1024),
    )(returned, grad_output)


def per_device(signal, gate_values, filter_taps, skip_gain, grad_output):
    groups = lax.axis_size("wide") * lax.axis_size("narrow")
    seq_rows, channels = signal.shape
    own = channels // groups
    fits = groups <= 32 and groups % 4 == 0 and seq_rows == LANES
    fits = fits and lax.axis_size("parts") == 2
    if fits and own >= CHUNK and own % CHUNK == 0 and channels % LANES == 0:
        return per_device_fused(signal, gate_values, filter_taps, skip_gain, grad_output)
    return per_device_plain(signal, gate_values, filter_taps, skip_gain, grad_output)


def solution(mesh):
    placed = (
        P(("parts", "wide", "narrow"), None),
        P(("parts", "wide", "narrow"), None),
        P(("wide", "narrow"), None),
        P(("wide", "narrow")),
        P(("parts", "wide", "narrow"), None),
    )
    return jax.shard_map(
        per_device,
        mesh=mesh,
        in_specs=placed,
        out_specs=(
            P(("parts", "wide", "narrow"), None),
            P(("parts", "wide", "narrow"), None),
            P(("parts", "wide", "narrow"), None),
        ),
        check_vma=False,
    )
```

```python
import functools
import math

import jax
import jax.numpy as jnp
import numpy as np
from jax import lax
from jax.experimental import pallas as pl
from jax.experimental.pallas import tpu as pltpu
from jax.sharding import PartitionSpec as P

precise = lax.Precision.HIGHEST


def angle_tables(left_count, right_count, period):
    left_index = jnp.arange(left_count, dtype=jnp.int32)
    right_index = jnp.arange(right_count, dtype=jnp.int32)
    phases = left_index[:, None] * right_index[None, :] % period
    angles = phases.astype(jnp.float32) * (2.0 * math.pi / period)
    return (jnp.cos(angles), jnp.sin(angles))


def spectral_tables(groups, seq_rows):
    full_span = 2 * groups * seq_rows
    outer_cos, outer_sin = angle_tables(2 * groups, groups, 2 * groups)
    twist_cos, twist_sin = angle_tables(2 * groups, seq_rows, full_span)
    inner_cos, inner_sin = angle_tables(seq_rows, seq_rows, seq_rows)
    return (outer_cos, outer_sin, twist_cos, twist_sin, inner_cos, inner_sin, full_span)


def transform(field, tables):
    outer_cos, outer_sin, twist_cos, twist_sin, inner_cos, inner_sin, full_span = tables
    first_real = jnp.einsum("ka,ucab->uckb", outer_cos, field, precision=precise)
    first_imag = -jnp.einsum("ka,ucab->uckb", outer_sin, field, precision=precise)
    turned_real = first_real * twist_cos + first_imag * twist_sin
    turned_imag = first_imag * twist_cos - first_real * twist_sin
    spec_real = jnp.einsum("uckb,bj->uckj", turned_real, inner_cos, precision=precise) + jnp.einsum(
        "uckb,bj->uckj", turned_imag, inner_sin, precision=precise
    )
    spec_imag = jnp.einsum("uckb,bj->uckj", turned_imag, inner_cos, precision=precise) - jnp.einsum(
        "uckb,bj->uckj", turned_real, inner_sin, precision=precise
    )
    return (spec_real, spec_imag)


def untwist(spec_real, spec_imag, tables):
    outer_cos, outer_sin, twist_cos, twist_sin, inner_cos, inner_sin, full_span = tables
    back_real = jnp.einsum("uckj,bj->uckb", spec_real, inner_cos, precision=precise) - jnp.einsum(
        "uckj,bj->uckb", spec_imag, inner_sin, precision=precise
    )
    back_imag = jnp.einsum("uckj,bj->uckb", spec_imag, inner_cos, precision=precise) + jnp.einsum(
        "uckj,bj->uckb", spec_real, inner_sin, precision=precise
    )
    turned_real = back_real * twist_cos - back_imag * twist_sin
    turned_imag = back_imag * twist_cos + back_real * twist_sin
    return (turned_real, turned_imag)


def inverse_real(spec_real, spec_imag, tables):
    outer_cos, outer_sin = (tables[0], tables[1])
    factor = 1.0 / tables[6]
    turned_real, turned_imag = untwist(spec_real, spec_imag, tables)
    out_real = jnp.einsum("ka,uckb->ucab", outer_cos, turned_real, precision=precise) - jnp.einsum(
        "ka,uckb->ucab", outer_sin, turned_imag, precision=precise
    )
    return out_real * factor


def to_channels(stacked, wide_count, narrow_count):
    stack_count, channels, seq_rows = stacked.shape
    groups = wide_count * narrow_count
    own_channels = channels // groups
    arrived = lax.all_to_all(stacked, ("wide", "narrow"), split_axis=1, concat_axis=2, tiled=True)
    return arrived.reshape(stack_count, own_channels, groups, seq_rows)


def to_sequence(field):
    stack_count, own_channels, groups, seq_rows = field.shape
    flat_field = field.reshape(stack_count, own_channels, groups * seq_rows)
    arrived = lax.all_to_all(
        flat_field, ("wide", "narrow"), split_axis=2, concat_axis=1, tiled=True
    )
    return arrived


def backward_channels(
    inner_chan,
    inner_real,
    inner_imag,
    signal_real,
    signal_imag,
    taps_real,
    taps_imag,
    skip_gain,
    tables,
    total_rows,
):
    taps_side_real = inner_real * taps_real + inner_imag * taps_imag
    taps_side_imag = inner_imag * taps_real - inner_real * taps_imag
    signal_side_real = inner_real * signal_real + inner_imag * signal_imag
    signal_side_imag = inner_imag * signal_real - inner_real * signal_imag
    back_taps = inverse_real(taps_side_real, taps_side_imag, tables)
    back_signal = inverse_real(signal_side_real, signal_side_imag, tables)
    signal_chan = (back_taps[0] + skip_gain[:, None, None] * inner_chan[0]).astype(jnp.bfloat16)
    filter_chan = (back_signal[0] * (1.0 / math.sqrt(total_rows))).astype(jnp.bfloat16)
    return (signal_chan, filter_chan)


def per_device_plain(signal, gate_values, filter_taps, skip_gain, grad_output):
    wide_count = lax.axis_size("wide")
    narrow_count = lax.axis_size("narrow")
    groups = wide_count * narrow_count
    seq_rows = signal.shape[0]
    total_rows = groups * seq_rows
    tables = spectral_tables(groups, seq_rows)
    grad_vals = grad_output.astype(jnp.float32)
    paired = jnp.stack([jnp.transpose(signal), jnp.transpose(filter_taps)])
    spread_pair = to_channels(paired, wide_count, narrow_count).astype(jnp.float32)
    pair_real, pair_imag = transform(spread_pair, tables)
    signal_real, signal_imag = (pair_real[0:1], pair_imag[0:1])
    taps_real, taps_imag = (pair_real[1:2], pair_imag[1:2])
    conv_real = signal_real * taps_real - signal_imag * taps_imag
    conv_imag = signal_real * taps_imag + signal_imag * taps_real
    convolved = inverse_real(conv_real, conv_imag, tables)[0]
    mixed_chan = (convolved + skip_gain[:, None, None] * spread_pair[0]).astype(jnp.bfloat16)
    mixed_rows = jnp.transpose(to_sequence(mixed_chan[None])[0])
    gate_grad = (grad_vals * mixed_rows.astype(jnp.float32)).astype(jnp.bfloat16)
    inner_grad = (grad_vals * gate_values.astype(jnp.float32)).astype(jnp.bfloat16)
    inner_chan = to_channels(jnp.transpose(inner_grad)[None], wide_count, narrow_count).astype(
        jnp.float32
    )
    inner_real, inner_imag = transform(inner_chan, tables)
    signal_chan, filter_chan = backward_channels(
        inner_chan,
        inner_real,
        inner_imag,
        signal_real,
        signal_imag,
        taps_real,
        taps_imag,
        skip_gain,
        tables,
        total_rows,
    )
    returned = to_sequence(jnp.stack([signal_chan, filter_chan]))
    signal_grad = jnp.transpose(returned[0])
    filter_grad = jnp.transpose(returned[1])
    return (signal_grad, gate_grad, filter_grad)


LANES = 128
CHUNK = 16
MESH = pl.DeviceIdType.MESH


def fused_tables(groups, seq_rows):
    span = 2 * groups * seq_rows
    kept = np.arange(groups + 1)[:, None]
    turn = 2.0 * np.pi * (kept * np.arange(seq_rows)[None, :]) / span
    weight = np.where((kept == 0) | (kept == groups), 1.0, 2.0) / span
    twist = np.stack([np.cos(turn), np.sin(turn), weight * np.cos(turn), weight * np.sin(turn)])
    index = np.arange(seq_rows)
    angle = 2.0 * np.pi * (index[:, None] * index[None, :] % seq_rows) / seq_rows
    cos, sin = np.cos(angle), np.sin(angle)
    ahead = np.block([[cos, -sin], [sin, cos]]).astype(np.float32)
    both = []
    for table in (ahead, ahead.T):
        high = table.astype(jnp.bfloat16)
        both += [high, (table - high.astype(np.float32)).astype(jnp.bfloat16)]
    return twist.astype(np.float32), np.stack(both)


def weighted_sum(pairs):
    by_size = {}
    for coefficient, array in pairs:
        if abs(coefficient) > 1e-9:
            key = round(abs(coefficient), 9)
            by_size.setdefault(key, (abs(coefficient), []))[1].append((coefficient > 0, array))
    total = None
    for size, members in by_size.values():
        members = sorted(members, key=lambda member: not member[0])
        positive = members[0][0]
        partial = members[0][1]
        for sign, array in members[1:]:
            partial = partial + array if sign == positive else partial - array
        factor = 1.0 if abs(size - 1.0) < 1e-9 else size
        if factor != 1.0:
            partial = partial * np.float32(factor)
        if total is None:
            total = partial if positive else -partial
        else:
            total = total + partial if positive else total - partial
    return total


def add(left, right):
    if left is None or right is None:
        return right if left is None else left
    return left + right


def sub(left, right):
    if left is None:
        return None if right is None else -right
    return left if right is None else left - right


def outer_forward(x):
    groups = len(x)
    half = groups // 2
    unit = math.pi / groups
    plus = {a: x[a] + x[groups - a] for a in range(1, half)}
    minus = {a: x[a] - x[groups - a] for a in range(1, half)}
    real, imag = [None] * (groups + 1), [None] * (groups + 1)
    for k in range(half + 1):
        even = k % 2 == 0
        cos_side, sin_side = (plus, minus) if even else (minus, plus)
        cos_parts, sin_parts = [[(1.0, x[0])], []], [[], []]
        cos_parts[half % 2].append((math.cos(unit * k * half), x[half]))
        sin_parts[half % 2].append((math.sin(unit * k * half), x[half]))
        for a in range(1, half):
            cos_parts[a % 2].append((math.cos(unit * k * a), cos_side[a]))
            sin_parts[a % 2].append((math.sin(unit * k * a), sin_side[a]))
        cos_even, cos_odd = weighted_sum(cos_parts[0]), weighted_sum(cos_parts[1])
        sin_even, sin_odd = weighted_sum(sin_parts[0]), weighted_sum(sin_parts[1])
        real[k] = add(cos_even, cos_odd)
        imag[k] = sub(sub(None, sin_even), sin_odd)
        real[groups - k] = sub(cos_even, cos_odd)
        if k < half:
            imag[groups - k] = sub(sin_even, sin_odd)
    zero = jnp.zeros_like(x[0])
    return [zero if v is None else v for v in real], [zero if v is None else v for v in imag]


def outer_inverse(real, imag):
    groups = len(real) - 1
    half = groups // 2
    unit = math.pi / groups
    out = [None] * groups
    for a_parity in (0, 1):
        cos_side, sin_side = {}, {}
        for k in range(1, half):
            if a_parity == 0:
                cos_side[k] = real[k] + real[groups - k]
                sin_side[k] = imag[k] - imag[groups - k]
            else:
                cos_side[k] = real[k] - real[groups - k]
                sin_side[k] = imag[k] + imag[groups - k]
        ends = real[0] + real[groups] if a_parity == 0 else real[0] - real[groups]
        for a in range(a_parity, half + 1, 2):
            cos_parts, sin_parts = [[(1.0, ends)], []], [[], []]
            cos_parts[half % 2].append((math.cos(unit * half * a), real[half]))
            sin_parts[half % 2].append((math.sin(unit * half * a), imag[half]))
            for k in range(1, half):
                cos_parts[k % 2].append((math.cos(unit * k * a), cos_side[k]))
                sin_parts[k % 2].append((math.sin(unit * k * a), sin_side[k]))
            cos_even, cos_odd = weighted_sum(cos_parts[0]), weighted_sum(cos_parts[1])
            sin_even, sin_odd = weighted_sum(sin_parts[0]), weighted_sum(sin_parts[1])
            out[a] = sub(sub(add(cos_even, cos_odd), sin_even), sin_odd)
            if 0 < a < half:
                out[groups - a] = sub(add(sub(cos_even, cos_odd), sin_even), sin_odd)
    return out


def split(value):
    high = value.astype(jnp.bfloat16)
    return high, (value - high.astype(jnp.float32)).astype(jnp.bfloat16)


def fused_kernel(
    groups,
    narrow_count,
    total_rows,
    signal_hbm,
    gate_hbm,
    taps_hbm,
    skip_hbm,
    grad_hbm,
    twist_hbm,
    inner_hbm,
    returned,
    signal_ref,
    gate_ref,
    taps_ref,
    skip_ref,
    grad_ref,
    twist_ref,
    inner_ref,
    outgoing,
    arrived,
    results,
    high_ref,
    low_ref,
    spec_ref,
    out_send,
    out_recv,
    back_send,
    back_recv,
    local_sem,
    load_sem,
):
    seq_rows, channels = signal_ref.shape
    own = channels // groups
    chunks = own // CHUNK
    part = lax.axis_index("parts")
    me = lax.axis_index("wide") * narrow_count + lax.axis_index("narrow")

    def device(index):
        return (part, index // narrow_count, index % narrow_count)

    barrier = pltpu.get_barrier_semaphore()
    pairs = [
        (signal_hbm, signal_ref),
        (taps_hbm, taps_ref),
        (grad_hbm, grad_ref),
        (gate_hbm, gate_ref),
        (skip_hbm, skip_ref),
        (twist_hbm, twist_ref),
        (inner_hbm, inner_ref),
    ]
    loads = [
        pltpu.make_async_copy(far, near, load_sem.at[i]) for i, (far, near) in enumerate(pairs)
    ]
    for load in loads:
        load.start()

    def greet(step, carry):
        pl.semaphore_signal(
            barrier, inc=1, device_id=device((me + step) % groups), device_id_type=MESH
        )
        return carry

    lax.fori_loop(1, groups, greet, 0)

    for load in loads[:4]:
        load.wait()
    for first in range(0, channels, LANES):
        columns = slice(first, first + LANES)
        grad_vals = grad_ref[:, columns].astype(jnp.float32)
        inner = (grad_vals * gate_ref[:, columns].astype(jnp.float32)).astype(jnp.bfloat16)
        outgoing[0, columns, :] = signal_ref[:, columns].T
        outgoing[1, columns, :] = taps_ref[:, columns].T
        outgoing[2, columns, :] = inner.T
    pl.semaphore_wait(barrier, groups - 1)

    def rows_of(index, chunk):
        return pl.ds(pl.multiple_of(index * own + chunk * CHUNK, CHUNK), CHUNK)

    def chunk_rows(chunk):
        return pl.ds(pl.multiple_of(chunk * CHUNK, CHUNK), CHUNK)

    def spread(chunk, step):
        other = (me + step) % groups
        return pltpu.make_async_remote_copy(
            src_ref=outgoing.at[:, rows_of(other, chunk), :],
            dst_ref=arrived.at[me, :, chunk_rows(chunk), :],
            send_sem=out_send.at[chunk, step],
            recv_sem=out_recv.at[chunk, step],
            device_id=device(other),
            device_id_type=MESH,
        )

    def bring(chunk, step):
        other = (me + step) % groups
        return pltpu.make_async_remote_copy(
            src_ref=results.at[other, :, chunk_rows(chunk), :],
            dst_ref=returned.at[:, rows_of(me, chunk), :],
            send_sem=back_send.at[chunk, step],
            recv_sem=back_recv.at[chunk, step],
            device_id=device(other),
            device_id_type=MESH,
        )

    for chunk in range(chunks):

        def start(step, carry, chunk=chunk):
            spread(chunk, (step + groups // 2 - 2) % (groups - 1) + 1).start()
            return carry

        lax.fori_loop(1, groups, start, 0)
    keep = pltpu.make_async_copy(
        outgoing.at[:, pl.ds(pl.multiple_of(me * own, CHUNK), own), :],
        arrived.at[me],
        local_sem,
    )
    keep.start()

    for load in loads[4:]:
        load.wait()
    lane = lax.broadcasted_iota(jnp.int32, (own, own), 1)
    row = lax.broadcasted_iota(jnp.int32, (own, own), 0)
    gain_all = jnp.sum(
        jnp.where(lane == row, jnp.broadcast_to(skip_ref[...], (own, own)), 0.0),
        axis=1,
        keepdims=True,
    )
    keep.wait()

    kept = groups + 1
    size = kept * 3 * CHUNK

    def inner_transform(which):
        high = high_ref[...].reshape(size, 2 * seq_rows)
        low = low_ref[...].reshape(size, 2 * seq_rows)
        table_high, table_low = inner_ref[which], inner_ref[which + 1]
        dot = functools.partial(jnp.dot, preferred_element_type=jnp.float32)
        total = dot(high, table_high) + dot(high, table_low) + dot(low, table_high)
        spec_ref[...] = total.reshape(kept, 3, CHUNK, 2 * seq_rows)

    def store_pair(k, u, real, imag):
        real_high, real_low = split(real)
        imag_high, imag_low = split(imag)
        high_ref[k, u, :, :seq_rows] = real_high
        high_ref[k, u, :, seq_rows:] = imag_high
        low_ref[k, u, :, :seq_rows] = real_low
        low_ref[k, u, :, seq_rows:] = imag_low

    for chunk in range(chunks):
        rows = slice(chunk * CHUNK, (chunk + 1) * CHUNK)

        def await_in(step, carry, chunk=chunk):
            spread(chunk, step).wait_recv()
            return carry

        lax.fori_loop(1, groups, await_in, 0)

        def ahead(u, carry, rows=rows):
            blocks = [arrived[a, u, rows, :].astype(jnp.float32) for a in range(groups)]
            real, imag = outer_forward(blocks)
            for k in range(kept):
                cos, sin = twist_ref[0, k : k + 1, :], twist_ref[1, k : k + 1, :]
                store_pair(
                    k, u, real[k] * cos + imag[k] * sin, imag[k] * cos - real[k] * sin
                )
            return carry

        lax.fori_loop(0, 3, ahead, 0)
        inner_transform(0)

        def multiply(k, carry):
            parts = [
                (spec_ref[k, u, :, :seq_rows], spec_ref[k, u, :, seq_rows:]) for u in range(3)
            ]
            (s_re, s_im), (t_re, t_im), (i_re, i_im) = parts
            store_pair(k, 0, s_re * t_re - s_im * t_im, s_re * t_im + s_im * t_re)
            store_pair(k, 1, i_re * t_re + i_im * t_im, i_im * t_re - i_re * t_im)
            store_pair(k, 2, i_re * s_re + i_im * s_im, i_im * s_re - i_re * s_im)
            return carry

        lax.fori_loop(0, kept, multiply, 0)
        inner_transform(2)

        gain = gain_all[rows, :]

        def back(u, carry, rows=rows, gain=gain):
            real, imag = [], []
            for k in range(kept):
                re, im = spec_ref[k, u, :, :seq_rows], spec_ref[k, u, :, seq_rows:]
                cos, sin = twist_ref[2, k : k + 1, :], twist_ref[3, k : k + 1, :]
                real.append(re * cos - im * sin)
                imag.append(im * cos + re * sin)
            for a, block in enumerate(outer_inverse(real, imag)):
                skipped = arrived[a, 2 * u, rows, :].astype(jnp.float32)
                results[a, u, rows, :] = (block + gain * skipped).astype(jnp.bfloat16)
            return carry

        lax.fori_loop(0, 2, back, 0)
        real, imag = [], []
        for k in range(kept):
            re, im = spec_ref[k, 2, :, :seq_rows], spec_ref[k, 2, :, seq_rows:]
            cos, sin = twist_ref[2, k : k + 1, :], twist_ref[3, k : k + 1, :]
            real.append(re * cos - im * sin)
            imag.append(im * cos + re * sin)
        for a, block in enumerate(outer_inverse(real, imag)):
            scaled = block * np.float32(1.0 / math.sqrt(total_rows))
            results[a, 2, rows, :] = scaled.astype(jnp.bfloat16)

        def start_back(step, carry, chunk=chunk):
            bring(chunk, (step + groups // 2 - 2) % (groups - 1) + 1).start()
            return carry

        lax.fori_loop(1, groups, start_back, 0)

    mine = pltpu.make_async_copy(
        results.at[me],
        returned.at[:, pl.ds(pl.multiple_of(me * own, CHUNK), own), :],
        local_sem,
    )
    mine.start()
    mine.wait()
    for chunk in range(chunks):

        def finish(step, carry, chunk=chunk):
            bring(chunk, step).wait_recv()
            return carry

        lax.fori_loop(1, groups, finish, 0)

    for chunk in range(chunks):

        def drain(step, carry, chunk=chunk):
            spread(chunk, step).wait_send()
            bring(chunk, step).wait_send()
            return carry

        lax.fori_loop(1, groups, drain, 0)


def tokens_kernel(
    returned_hbm,
    grad_hbm,
    signal_out,
    gate_out,
    filter_out,
    returned,
    grad_ref,
    staged,
    load_sems,
    sems,
):
    outs = (signal_out, gate_out, filter_out)
    copies = []
    spans = [slice(first, first + LANES) for first in range(0, grad_ref.shape[1], LANES)]
    grad_load = pltpu.make_async_copy(grad_hbm, grad_ref, load_sems.at[len(spans)])
    grad_load.start()
    loads = [
        pltpu.make_async_copy(
            returned_hbm.at[:, columns, :], returned.at[:, columns, :], load_sems.at[block]
        )
        for block, columns in enumerate(spans)
    ]
    for load in loads:
        load.start()
    grad_load.wait()
    for block, columns in enumerate(spans):
        loads[block].wait()
        mixed = returned[0, columns, :].T.astype(jnp.float32)
        staged[0, :, columns] = returned[1, columns, :].T
        staged[1, :, columns] = (grad_ref[:, columns].astype(jnp.float32) * mixed).astype(
            jnp.bfloat16
        )
        staged[2, :, columns] = returned[2, columns, :].T
        for u in range(3):
            copies.append(
                pltpu.make_async_copy(
                    staged.at[u, :, columns], outs[u].at[:, columns], sems.at[block, u]
                )
            )
            copies[-1].start()
    for copy in copies:
        copy.wait()


def per_device_fused(signal, gate_values, filter_taps, skip_gain, grad_output):
    narrow_count = lax.axis_size("narrow")
    groups = lax.axis_size("wide") * narrow_count
    seq_rows, channels = signal.shape
    own = channels // groups
    chunks = own // CHUNK
    twist, inner = fused_tables(groups, seq_rows)
    far = pl.BlockSpec(memory_space=pl.ANY)
    rows = (groups + 1, 3, CHUNK, 2 * seq_rows)
    operands = (
        signal,
        gate_values,
        filter_taps,
        skip_gain[None, :],
        grad_output,
        jnp.asarray(twist),
        jnp.asarray(inner),
    )
    returned = pl.pallas_call(
        functools.partial(fused_kernel, groups, narrow_count, groups * seq_rows),
        out_shape=jax.ShapeDtypeStruct((3, channels, seq_rows), jnp.bfloat16),
        in_specs=[far] * len(operands),
        out_specs=far,
        scratch_shapes=[
            *[pltpu.VMEM(operand.shape, operand.dtype) for operand in operands],
            pltpu.VMEM((3, channels, seq_rows), jnp.bfloat16),
            pltpu.VMEM((groups, 3, own, seq_rows), jnp.bfloat16),
            pltpu.VMEM((groups, 3, own, seq_rows), jnp.bfloat16),
            pltpu.VMEM(rows, jnp.bfloat16),
            pltpu.VMEM(rows, jnp.bfloat16),
            pltpu.VMEM(rows, jnp.float32),
            pltpu.SemaphoreType.DMA((chunks, groups)),
            pltpu.SemaphoreType.DMA((chunks, groups)),
            pltpu.SemaphoreType.DMA((chunks, groups)),
            pltpu.SemaphoreType.DMA((chunks, groups)),
            pltpu.SemaphoreType.DMA,
            pltpu.SemaphoreType.DMA((len(operands),)),
        ],
        compiler_params=pltpu.CompilerParams(
            collective_id=0, has_side_effects=True, vmem_limit_bytes=56 * 1024 * 1024
        ),
    )(*operands)
    shape = jax.ShapeDtypeStruct((seq_rows, channels), jnp.bfloat16)
    return pl.pallas_call(
        tokens_kernel,
        out_shape=(shape, shape, shape),
        in_specs=[far, far],
        out_specs=(far, far, far),
        scratch_shapes=[
            pltpu.VMEM((3, channels, seq_rows), jnp.bfloat16),
            pltpu.VMEM((seq_rows, channels), jnp.bfloat16),
            pltpu.VMEM((3, seq_rows, channels), jnp.bfloat16),
            pltpu.SemaphoreType.DMA((channels // LANES + 1,)),
            pltpu.SemaphoreType.DMA((channels // LANES, 3)),
        ],
        compiler_params=pltpu.CompilerParams(vmem_limit_bytes=56 * 1024 * 1024),
    )(returned, grad_output)


def per_device(signal, gate_values, filter_taps, skip_gain, grad_output):
    groups = lax.axis_size("wide") * lax.axis_size("narrow")
    seq_rows, channels = signal.shape
    own = channels // groups
    fits = groups <= 32 and groups % 4 == 0 and seq_rows == LANES
    if fits and own >= CHUNK and own % CHUNK == 0 and channels % LANES == 0:
        return per_device_fused(signal, gate_values, filter_taps, skip_gain, grad_output)
    return per_device_plain(signal, gate_values, filter_taps, skip_gain, grad_output)


def solution(mesh):
    placed = (
        P(("parts", "wide", "narrow"), None),
        P(("parts", "wide", "narrow"), None),
        P(("wide", "narrow"), None),
        P(("wide", "narrow")),
        P(("parts", "wide", "narrow"), None),
    )
    return jax.shard_map(
        per_device,
        mesh=mesh,
        in_specs=placed,
        out_specs=(
            P(("parts", "wide", "narrow"), None),
            P(("parts", "wide", "narrow"), None),
            P(("parts", "wide", "narrow"), None),
        ),
        check_vma=False,
    )
```
